256 devices in a mesh: seq: 16 (over x_lo, z), head: 16 (over y, x_hi, core).
Axes of the slice: x: 4 (x_hi: 2, x_lo: 2; x = x_hi * 2 + x_lo), y: 4, z: 8, core: 2. Of those that a mesh axis runs over, the one named last changes fastest.
Arguments:
- hidden_in: bfloat16 [4096, 7168], P('seq', 'head'), may hold values from -6 to 6
- w_qa: bfloat16 [7168, 1536], P('head'), may hold values from -0.0625 to 0.0625
- w_kva: bfloat16 [7168, 576], P('head'), may hold values from -0.0625 to 0.0625
- q_norm_gain: float32 [1536], replicated, may hold values from 0.5 to 10
- kv_norm_gain: float32 [512], replicated, may hold values from 0.5 to 10
- w_qb: bfloat16 [1536, 12288], P(None, 'head'), may hold values from -0.15625 to 0.15625
- w_uk: bfloat16 [64, 128, 512], P('head'), may hold values from -0.25 to 0.25
- value_up_weight: bfloat16 [64, 512, 128], P('head'), may hold values from -0.25 to 0.25
- positions: int32 [4096], P('seq'), may hold values from 0 to 4095, as said below
Outputs:
- head_values: bfloat16 [4096, 8192], P('seq', 'head')
The draws below stay inside these ranges and needn't reach their ends.
Inputs may be any that keep to these rules, and one draw needn't show every extreme that they name: A permutation of 0 to 4095 made of aligned runs of 128 rows, each run holding consecutive positions in rising order.
All inputs are finite; a program needn't handle non-finite values.
Results may differ from the reference program's by a relative error of at most 0.025.
The reference program's roundings to bfloat16 on the way count: a program that leaves them out, or rounds other values in their place, can miss the bound.
Values may be sent and summed in bfloat16 or wider, within the bound.
A program may use at most 64 MiB of HBM per device.

```python
import jax
import jax.numpy as jnp
from jax import lax

D = 7168
HEADS = 64
QL = 1536
KL = 512
ROPE = 64
NOPE = 128
VD = 128
TOK_DEV = 256
TOKENS = 4096


def draw_positions(key, part):
    key = jax.random.fold_in(key, 7)
    half_rows = TOK_DEV // 2
    running_count = TOKENS // half_rows
    order = jax.random.permutation(key, running_count)
    index = jnp.arange(TOKENS)
    return (order[index // half_rows] * half_rows + index % half_rows).astype(jnp.int32)


def gain_values(key, length):
    return jnp.exp(jax.random.uniform(key, (length,), jnp.float32, -0.69, 0.69))


def draw_q_norm_gain(key, part):
    key = jax.random.fold_in(key, 11)
    return gain_values(key, QL)


def draw_kv_norm_gain(key, part):
    key = jax.random.fold_in(key, 13)
    return gain_values(key, KL)


def levels(stream_key, dims, shards, low, high):
    gain, own = 1.0, jax.random.fold_in(stream_key, 6)
    for axis_at, shards_of in shards:
        heights = jnp.exp(jax.random.uniform(jax.random.fold_in(own, axis_at), (shards_of,), jnp.float32, low / len(shards), high / len(shards)))
        gain = gain * jnp.repeat(heights, dims[axis_at] // shards_of).reshape([-1 if axis == axis_at else 1 for axis in range(len(dims))])
    return gain


def gaussian(own_key, extent, scale, most, cuts=(), kind=jnp.bfloat16):
    values = scale * jax.random.normal(own_key, extent, jnp.float32)
    if cuts:
        values = values * levels(own_key, extent, cuts, -0.22, 0.18)
    return jnp.clip(values, -most, most).astype(kind)


def setup_inputs(seed: int = 0) -> dict:
    seeds = jax.random.split(jax.random.key(seed), 10)
    return {
        "hidden_in": gaussian(seeds[0], (TOKENS, D), 1.0, 6.0, ((0, 16), (1, 16))),
        "w_qa": gaussian(seeds[1], (D, QL), D ** -0.5, 0.0625, ((0, 16),)),
        "w_kva": gaussian(seeds[2], (D, KL + ROPE), D ** -0.5, 0.0625, ((0, 16),)),
        "q_norm_gain": draw_q_norm_gain(jax.random.fold_in(seeds[9], 71), 0),
        "kv_norm_gain": draw_kv_norm_gain(jax.random.fold_in(seeds[9], 71), 0),
        "w_qb": gaussian(seeds[5], (QL, HEADS * (NOPE + ROPE)), QL ** -0.5, 0.15625, ((1, 16),)),
        "w_uk": gaussian(seeds[6], (HEADS, NOPE, KL), KL ** -0.5, 0.25, ((0, 16),)),
        "value_up_weight": gaussian(seeds[7], (HEADS, KL, VD), KL ** -0.5, 0.25, ((0, 16),)),
        "positions": draw_positions(jax.random.fold_in(seeds[9], 71), 0),
    }


def frequencies(positions):
    exponent = jnp.arange(0, ROPE, 2).astype(jnp.float32) / ROPE
    inverse = 50000.0 ** (-exponent)
    return positions.astype(jnp.float32)[:, None] * inverse[None, :]

def rotate(vector, cosine, sine):
    width = vector.shape[-1] // 2
    first = vector[..., :width]
    second = vector[..., width:]
    return jnp.concatenate([first * cosine - second * sine, second * cosine + first * sine], -1)

def rms_norm(vector, norm_gain):
    return vector * lax.rsqrt(lax.optimization_barrier(jnp.mean(vector * vector, -1, keepdims=True)) + 1e-06) * norm_gain

def reference(hidden_in, w_qa, w_kva, q_norm_gain, kv_norm_gain, w_qb, w_uk, value_up_weight, positions):
    q_low = jnp.dot(hidden_in, w_qa, preferred_element_type=jnp.float32)
    key_value_latent = jnp.dot(hidden_in, w_kva, preferred_element_type=jnp.float32)
    angles = frequencies(positions)
    cosine = jnp.cos(angles)
    sine = jnp.sin(angles)
    c_q = rms_norm(q_low, q_norm_gain).astype(jnp.bfloat16)
    keys = jnp.concatenate([rms_norm(key_value_latent[:, :KL], kv_norm_gain), rotate(key_value_latent[:, KL:], cosine, sine)], 1).astype(jnp.bfloat16)
    expanded_keys = keys.astype(jnp.float32)
    scale = 1.0 / (NOPE + ROPE) ** 0.5
    block_rows = min(64, TOKENS)

    def one_block(block_index):
        first = (block_index * block_rows).astype(jnp.int32)
        query_rows = lax.dynamic_slice_in_dim(c_q, first, block_rows, 0)
        query_pos = lax.dynamic_slice_in_dim(positions, first, block_rows, 0)
        block_cos = lax.dynamic_slice_in_dim(cosine, first, block_rows, 0)[:, None, :]
        block_sin = lax.dynamic_slice_in_dim(sine, first, block_rows, 0)[:, None, :]
        query = jnp.dot(query_rows, w_qb, preferred_element_type=jnp.float32).astype(jnp.bfloat16)
        query = query.reshape(block_rows, HEADS, NOPE + ROPE)
        q_rot = rotate(query[..., NOPE:].astype(jnp.float32), block_cos, block_sin).astype(jnp.bfloat16)
        q_lat = jnp.einsum('thn,hnk->thk', query[..., :NOPE].astype(jnp.float32), w_uk.astype(jnp.float32)).astype(jnp.bfloat16)
        joined = jnp.concatenate([q_lat, q_rot], -1).astype(jnp.float32)
        scores = jnp.einsum('thk,uk->thu', joined, expanded_keys) * scale
        allowed = positions[None, None, :] <= query_pos[:, None, None]
        scores = jnp.where(allowed, scores, -jnp.inf)
        probs = jax.nn.softmax(scores, -1).astype(jnp.bfloat16)
        latent_output = jnp.einsum('thu,uk->thk', probs.astype(jnp.float32), expanded_keys[:, :KL]).astype(jnp.bfloat16)
        value_rows = jnp.einsum('ale,led->ald', latent_output.astype(jnp.float32), value_up_weight.astype(jnp.float32)).astype(jnp.bfloat16)
        return value_rows.reshape(block_rows, HEADS * VD)
    result = lax.map(one_block, jnp.arange(TOKENS // block_rows))
    return result.reshape(TOKENS, HEADS * VD)
```

```python
import functools
import math

import jax
import jax.numpy as jnp
import numpy as np
from jax import lax
from jax.experimental import pallas as pl
from jax.experimental.pallas import tpu as pltpu
from jax.sharding import PartitionSpec as P

MESH = pl.DeviceIdType.MESH
F32 = jnp.float32
BF16 = jnp.bfloat16
I16 = jnp.int16
BIG = 2.0**100
KW = 640
QW = 1536 + 128


def place():
    s = lax.axis_index("seq")
    h = lax.axis_index("head")
    return h % 2, ((h // 2) % 2) * 2 + s // 8, h // 4, s % 8


def device(core, x, y, z):
    return ((x % 2) * 8 + z, y * 4 + (x // 2) * 2 + core)


def dot(a, b, over_a=1, over_b=0):
    return lax.dot_general(a, b, (((over_a,), (over_b,)), ((), ())), preferred_element_type=F32)


def encode(values, width):
    rows = values.shape[0]
    top = jnp.maximum(jnp.max(jnp.abs(values), -1, keepdims=True), 2.0**-60)
    level = jnp.ceil(jnp.log2(top) * 512.0)
    digits = jnp.round(values * (jnp.exp2(level * (-1.0 / 512.0)) * 32700.0))
    return digits.astype(jnp.int32).astype(I16), jnp.broadcast_to(level, (rows, width)).astype(jnp.int32).astype(I16)


def decode(digits, level):
    unit = jnp.exp2(level.astype(jnp.int32).astype(F32) * (1.0 / 512.0)) * (1.0 / 32700.0)
    return digits.astype(jnp.int32).astype(F32) * unit


def kernel(
    pos_ref, inv_row_ref, inv_col_ref, qg_ref, kg_ref, hid_hbm, wqa_hbm, wkv_hbm, wqb_hbm, uk_hbm, up_hbm,
    out_ref,
    hid_t, wqa_ref, wkv_ref, wqb_ref, uk_ref, up_ref, hid, uk_t, up_t,
    sx_kv, rx_kv, sx_q, rx_q, own_kv, own_q, st_kv, st_q, rs_kv, rs_q,
    cq_ref, key_ref, ke, vt, qt, s_ref, acc, m, l,
    send, recv, load,
):
    core, x, y, z = place()
    xh, xl = x // 2, x % 2
    j = y * 2 + xh
    p = x * (1 - core) + y * core
    q = y * (1 - core) + x * core
    used = [0]

    loads = []
    for i, (src, dst) in enumerate(
        ((hid_hbm, hid_t), (wkv_hbm, wkv_ref), (wqa_hbm, wqa_ref), (uk_hbm, uk_ref), (up_hbm, up_ref), (wqb_hbm, wqb_ref))
    ):
        loads.append(pltpu.make_async_copy(src, dst, load.at[i]))
        loads[-1].start()

    def copy(src, dst, target):
        at = used[0]
        used[0] += 1
        done = pltpu.make_async_remote_copy(
            src_ref=src, dst_ref=dst, send_sem=send.at[at], recv_sem=recv.at[at],
            device_id=target, device_id_type=MESH,
        )
        done.start()
        return done

    sibling = device(1 - core, x, y, z)
    peers = []
    for d in range(1, 8):
        py, px = (y + d // 2) % 4, (xh + d % 2) % 2
        peers.append((py * 2 + px, device(core, px * 2 + xl, py, z)))
    zs = [device(core, x, y, (z + d) % 8) for d in range(1, 8)]
    sides = [device(core, (x + d) % 4, y, z) for d in (1, 3)]
    barrier = pltpu.get_barrier_semaphore()
    greet = [sibling] + [who for _, who in peers] + zs + sides
    for who in greet:
        pl.semaphore_signal(barrier, inc=1, device_id=who, device_id_type=MESH)

    loads[0].wait()
    rows = hid_t[...].T
    for h in range(16):
        hid[h % 2, 16 * (h // 2) : 16 * (h // 2) + 16] = rows[16 * h : 16 * h + 16]
    other = hid[1 - core]
    mine = hid[core]
    loads[1].wait()
    digits, level = encode(dot(other, wkv_ref[...]), 64)
    sx_kv[:, :, :576] = digits.reshape(8, 16, 576)
    sx_kv[:, :, 576:] = level.reshape(8, 16, 64)
    pl.semaphore_wait(barrier, len(greet))
    c_kv = copy(sx_kv, rx_kv, sibling)
    loads[2].wait()
    digits, level = encode(dot(other, wqa_ref[...]), 128)
    sx_q[:, :, :1536] = digits.reshape(8, 16, 1536)
    sx_q[:, :, 1536:] = level.reshape(8, 16, 128)
    c_q = copy(sx_q, rx_q, sibling)
    own_kv[:, :, 576:] = jnp.zeros((8, 16, 64), F32)
    own_kv[:, :, :576] = dot(mine, wkv_ref[...]).reshape(8, 16, 576)
    own_q[...] = dot(mine, wqa_ref[...]).reshape(8, 16, 1536)

    c_kv.wait()
    low = own_kv[:, :, :576] + decode(rx_kv[:, :, :576], rx_kv[:, :, 576:577])
    own_kv[:, :, :576] = low
    digits, level = encode(low.reshape(128, 576), 64)
    st_kv[:, :, :576] = digits.reshape(8, 16, 576)
    st_kv[:, :, 576:] = level.reshape(8, 16, 64)
    p_kv = [copy(st_kv.at[pj], rs_kv.at[i], who) for i, (pj, who) in enumerate(peers)]
    c_q.wait()
    low = own_q[...] + decode(rx_q[:, :, :1536], rx_q[:, :, 1536:1537])
    own_q[...] = low
    digits, level = encode(low.reshape(128, 1536), 128)
    st_q[:, :, :1536] = digits.reshape(8, 16, 1536)
    st_q[:, :, 1536:] = level.reshape(8, 16, 128)
    p_q = [copy(st_q.at[pj], rs_q.at[i], who) for i, (pj, who) in enumerate(peers)]

    h = j * 2 + core
    base = pos_ref[128 * (h // 8)]
    run = base // 128
    tok = (base + (h % 8) * 16 + lax.broadcasted_iota(jnp.int32, (16, 128), 0)).astype(F32)
    lane = lax.broadcasted_iota(jnp.int32, (16, 128), 1)
    angle = tok * inv_row_ref[...]
    cosine, sine = jnp.cos(angle), jnp.sin(angle)
    tail = jnp.where(lane < 96, jnp.where(run > lane - 64, -BIG, 0.0), 0.0)
    loads[3].wait()
    loads[4].wait()
    for i in range(4):
        uk_t[:, 128 * i : 128 * i + 128] = uk_ref[i].T
        up_t[128 * i : 128 * i + 128, :] = up_ref[i].T
    for c in p_kv:
        c.wait()
    low = own_kv[j]
    parts = [decode(rs_kv[i, :, :576], rs_kv[i, :, 576:577]) for i in range(7)]
    latent = low[:, :512] + sum(part[:, :512] for part in parts)
    latent = latent * lax.rsqrt(jnp.mean(latent * latent, -1, keepdims=True) + 1e-06) * kg_ref[...].reshape(1, 512)
    key_ref[core, p, q, z, :, :512] = latent.astype(BF16)
    rope = sum(part[:, 512:576] for part in parts)
    rope = low[:, 512:] + jnp.concatenate([rope, jnp.zeros((16, 64), F32)], 1)
    swapped = jnp.where(lane < 32, -pltpu.roll(rope, 96, 1), pltpu.roll(rope, 32, 1))
    rope = jnp.where(lane < 64, rope * cosine + swapped * sine, tail)
    key_ref[core, p, q, z, :, 512:] = rope.astype(BF16)
    block = key_ref.at[core, p, q, z]
    p_z = [copy(block, block, who) for who in zs]

    for c in p_q:
        c.wait()
    low = own_q[j]
    for i in range(7):
        low = low + decode(rs_q[i, :, :1536], rs_q[i, :, 1536:1537])
    low = low * lax.rsqrt(jnp.mean(low * low, -1, keepdims=True) + 1e-06) * qg_ref[...].reshape(1, 1536)
    cq_ref[j, core] = low.astype(BF16)
    block = cq_ref.at[j, core]
    p_c = [copy(block, block, who) for _, who in peers]
    for c in p_z:
        c.wait()

    def slot(a, b, lo=0, hi=8):
        return key_ref.at[core, (p + a) % 4, (q + b) % 4, pl.ds(lo, hi - lo)]

    def to(a, b):
        return device(core, (x + a * (1 - core) + b * core) % 4, (y + a * core + b * (1 - core)) % 4, z)

    def ring(a, b, da, db):
        return [copy(slot(a, b), slot(a, b), to(da, db)), copy(slot(a, b), slot(a, b), to(3 * da, 3 * db))]

    def onward(pair, a, b, da, db):
        for c in pair:
            c.wait()
        left, right = slot(a + 3 * da, b + 3 * db, 0, 4), slot(a + da, b + db, 4, 8)
        return [copy(left, left, to(da, db)), copy(right, right, to(3 * da, 3 * db))]

    def share(a):
        line = key_ref.at[core, (p + a) % 4]
        return copy(line, line, sibling)

    first = ring(0, 0, 1, 0)
    lines = {0: ring(0, 0, 0, 1)}
    first = onward(first, 0, 0, 1, 0)
    lines[1] = ring(1, 0, 0, 1)
    lines[3] = ring(3, 0, 0, 1)
    lines[0] = onward(lines[0], 0, 0, 0, 1)
    for c in p_c:
        c.wait()
    mate = cq_ref.at[:, pl.ds(core, 1)]
    c_c = copy(mate, mate, sibling)
    for c in first:
        c.wait()
    lines[2] = ring(2, 0, 0, 1)

    def finish(a):
        for c in lines[a]:
            c.wait()
        return share(a)

    sp = y * (1 - core) + x * core

    def chunk(n):
        a = (0, 1, 3, 2)[n % 4]
        return (core, (p + a) % 4) if n < 4 else (1 - core, (sp + a) % 4)

    def expand(n):
        keys = key_ref[chunk(n)].reshape(512, KW)[:, :512]
        ke[n] = dot(keys, uk_t[...]).astype(BF16)
        vt[n] = dot(up_t[...], keys, 1, 1).astype(BF16)

    scale = math.log2(math.e) / math.sqrt(192)
    token = lax.broadcasted_iota(jnp.int32, (16, 256), 1)
    row = lax.broadcasted_iota(jnp.int32, (16, 256), 0)

    def attend(n):
        k, line = chunk(n)
        tails = key_ref[k, line].reshape(512, KW)[:, 512:]
        for i in range(4):
            s_ref[i] = dot(jnp.concatenate([ke[n, :, 128 * i : 128 * i + 128], tails], 1), qt[i])
        for b in range(4):
            kx = line * (1 - k) + b * k
            ky = b * (1 - k) + line * k
            key_token = (ky * 4 + (kx // 2) * 2 + k) * 16 + row
            hidden = (key_token > token) & (key_token // 128 == token // 128) & (kx % 2 == xl)
            strip = pl.ds(pl.multiple_of(b * 128 + z * 16, 16), 16)
            for i in range(4):
                s_ref[i, strip] = jnp.where(hidden, -BIG, s_ref[i, strip])
        for i in range(4):
            s = s_ref[i] * scale
            before = m[i]
            now = jnp.maximum(before, jnp.max(s, 0, keepdims=True))
            w = jnp.exp2(s - now)
            fade = jnp.exp2(before - now)
            l[i] = l[i] * fade + jnp.sum(w, 0, keepdims=True)
            m[i] = now
            acc[i] = acc[i] * fade + dot(vt[n, 128 * i : 128 * i + 128], w.astype(BF16))

    s_lines = {0: finish(0)}
    expand(0)
    m[...] = jnp.full(m.shape, -4 * BIG, F32)
    l[...] = jnp.zeros(l.shape, F32)
    acc[...] = jnp.zeros(acc.shape, F32)
    wide = lax.broadcasted_iota(jnp.int32, (32, 256), 1)
    base = jnp.where(wide < 128, pos_ref[0], pos_ref[128])
    angle = (base + wide % 128).astype(F32) * inv_col_ref[...]
    cosine, sine = jnp.cos(angle), jnp.sin(angle)
    runs = jnp.where(base // 128 == lax.broadcasted_iota(jnp.int32, (32, 256), 0), 1.0, 0.0).astype(BF16)
    loads[5].wait()
    c_c.wait()
    q_t = dot(cq_ref[...].reshape(256, 1536), wqb_ref[...]).astype(BF16).T
    for i in range(4):
        qt[i, :128] = q_t[192 * i : 192 * i + 128]
        a = q_t[192 * i + 128 : 192 * i + 160].astype(F32)
        b = q_t[192 * i + 160 : 192 * i + 192].astype(F32)
        qt[i, 128:160] = (a * cosine - b * sine).astype(BF16)
        qt[i, 160:192] = (b * cosine + a * sine).astype(BF16)
        qt[i, 192:224] = runs
        qt[i, 224:] = jnp.zeros((32, 256), BF16)
    s_lines[0].wait()
    expand(4)
    for a in (1, 3):
        lines[a] = onward(lines[a], a, 0, 0, 1)
    attend(0)
    attend(4)
    for a in (1, 3):
        s_lines[a] = finish(a)
    lines[2] = onward(lines[2], 2, 0, 0, 1)
    for n in (1, 2):
        expand(n)
        attend(n)
    s_lines[2] = finish(2)
    for n, a in ((5, 1), (6, 3)):
        s_lines[a].wait()
        expand(n)
        attend(n)
    expand(3)
    attend(3)
    s_lines[2].wait()
    expand(7)
    attend(7)
    for i in range(4):
        out_ref[:, 128 * i : 128 * i + 128] = (acc[i] / l[i]).T.astype(BF16)


def body(hidden_in, w_qa, w_kva, q_norm_gain, kv_norm_gain, w_qb, w_uk, value_up_weight, positions):
    inverse = 50000.0 ** (-np.arange(0, 64, 2) / 64)
    inv_row = np.zeros((1, 128), np.float32)
    inv_row[0, :32] = inverse
    inv_row[0, 32:64] = inverse
    inv_col = np.repeat(inverse.astype(np.float32)[:, None], 256, 1)
    vmem = pl.BlockSpec(memory_space=pltpu.VMEM)
    smem = pl.BlockSpec(memory_space=pltpu.SMEM)
    any_space = pl.BlockSpec(memory_space=pl.ANY)
    copies = 64
    return pl.pallas_call(
        kernel,
        name="attention",
        out_shape=jax.ShapeDtypeStruct((256, 512), BF16),
        in_specs=[smem] + [vmem] * 4 + [any_space] * 6,
        out_specs=vmem,
        scratch_shapes=[
            pltpu.VMEM((448, 256), BF16), pltpu.VMEM((448, 1536), BF16), pltpu.VMEM((448, 576), BF16),
            pltpu.VMEM((1536, 768), BF16), pltpu.VMEM((4, 128, 512), BF16), pltpu.VMEM((4, 512, 128), BF16),
            pltpu.VMEM((2, 128, 448), BF16), pltpu.VMEM((512, 512), BF16), pltpu.VMEM((512, 512), BF16),
            pltpu.VMEM((8, 16, KW), I16), pltpu.VMEM((8, 16, KW), I16),
            pltpu.VMEM((8, 16, QW), I16), pltpu.VMEM((8, 16, QW), I16),
            pltpu.VMEM((8, 16, KW), F32), pltpu.VMEM((8, 16, 1536), F32),
            pltpu.VMEM((8, 16, KW), I16), pltpu.VMEM((8, 16, QW), I16),
            pltpu.VMEM((7, 16, KW), I16), pltpu.VMEM((7, 16, QW), I16),
            pltpu.VMEM((8, 2, 16, 1536), BF16), pltpu.VMEM((2, 4, 4, 8, 16, KW), BF16),
            pltpu.VMEM((8, 512, 512), BF16), pltpu.VMEM((8, 512, 512), BF16),
            pltpu.VMEM((4, 256, 256), BF16), pltpu.VMEM((4, 512, 256), F32),
            pltpu.VMEM((4, 128, 256), F32), pltpu.VMEM((4, 1, 256), F32), pltpu.VMEM((4, 1, 256), F32),
            pltpu.SemaphoreType.DMA((copies,)), pltpu.SemaphoreType.DMA((copies,)), pltpu.SemaphoreType.DMA((6,)),
        ],
        compiler_params=pltpu.CompilerParams(
            collective_id=0, has_side_effects=True, vmem_limit_bytes=60 * 2**20
        ),
    )(
        positions, jnp.asarray(inv_row), jnp.asarray(inv_col), q_norm_gain, kv_norm_gain,
        hidden_in.T, w_qa, w_kva, w_qb, w_uk, value_up_weight,
    )


def solution(mesh):
    return jax.shard_map(
        body,
        mesh=mesh,
        in_specs=(
            P("seq", "head"), P("head", None), P("head", None), P(), P(), P(None, "head"),
            P("head", None, None), P("head", None, None), P("seq"),
        ),
        out_specs=P("seq", "head"),
        check_vma=False,
    )
```

```python
import functools
import math

import jax
import jax.numpy as jnp
import numpy as np
from jax import lax
from jax.experimental import pallas as pl
from jax.experimental.pallas import tpu as pltpu
from jax.sharding import PartitionSpec as P

MESH = pl.DeviceIdType.MESH
F32 = jnp.float32
BF16 = jnp.bfloat16
I16 = jnp.int16
BIG = 2.0**100
KW = 640
QW = 1536 + 128


def place():
    s = lax.axis_index("seq")
    h = lax.axis_index("head")
    return h % 2, ((h // 2) % 2) * 2 + s // 8, h // 4, s % 8


def device(core, x, y, z):
    return ((x % 2) * 8 + z, y * 4 + (x // 2) * 2 + core)


def dot(a, b, over_a=1, over_b=0):
    return lax.dot_general(a, b, (((over_a,), (over_b,)), ((), ())), preferred_element_type=F32)


def encode(values, width):
    rows = values.shape[0]
    top = jnp.maximum(jnp.max(jnp.abs(values), -1, keepdims=True), 2.0**-60)
    level = jnp.ceil(jnp.log2(top) * 512.0)
    digits = jnp.round(values * (jnp.exp2(level * (-1.0 / 512.0)) * 32700.0))
    return digits.astype(jnp.int32).astype(I16), jnp.broadcast_to(level, (rows, width)).astype(jnp.int32).astype(I16)


def decode(digits, level):
    unit = jnp.exp2(level.astype(jnp.int32).astype(F32) * (1.0 / 512.0)) * (1.0 / 32700.0)
    return digits.astype(jnp.int32).astype(F32) * unit


def kernel(
    pos_ref, inv_row_ref, inv_col_ref, qg_ref, kg_ref, hid_hbm, wqa_hbm, wkv_hbm, wqb_hbm, uk_hbm, up_hbm,
    out_ref,
    hid_t, wqa_ref, wkv_ref, wqb_ref, uk_ref, up_ref, hid, uk_t, up_t,
    sx_kv, rx_kv, sx_q, rx_q, own_kv, own_q, st_kv, st_q, rs_kv, rs_q,
    cq_ref, near_ref, far_ref, ke, vt, qt, s_ref, acc, m, l,
    send, recv, load,
):
    core, x, y, z = place()
    xh, xl = x // 2, x % 2
    j = y * 2 + xh
    p = x * (1 - core) + y * core
    q = y * (1 - core) + x * core
    used = [0]

    loads = []
    for i, (src, dst) in enumerate(
        ((hid_hbm, hid_t), (wkv_hbm, wkv_ref), (wqa_hbm, wqa_ref), (uk_hbm, uk_ref), (up_hbm, up_ref), (wqb_hbm, wqb_ref))
    ):
        loads.append(pltpu.make_async_copy(src, dst, load.at[i]))
        loads[-1].start()

    def copy(src, dst, target):
        at = used[0]
        used[0] += 1
        done = pltpu.make_async_remote_copy(
            src_ref=src, dst_ref=dst, send_sem=send.at[at], recv_sem=recv.at[at],
            device_id=target, device_id_type=MESH,
        )
        done.start()
        return done

    sibling = device(1 - core, x, y, z)
    peers = []
    for d in range(1, 8):
        py, px = (y + d // 2) % 4, (xh + d % 2) % 2
        peers.append((py * 2 + px, device(core, px * 2 + xl, py, z)))
    zs = [device(core, x, y, (z + d) % 8) for d in range(8)]
    plane = [device(core, (x + d % 4) % 4, (y + d // 4) % 4, z) for d in range(1, 16)]
    barrier = pltpu.get_barrier_semaphore()
    greet = [sibling] + zs[1:] + plane
    for who in greet:
        pl.semaphore_signal(barrier, inc=1, device_id=who, device_id_type=MESH)

    loads[0].wait()
    rows = hid_t[...].T
    for h in range(16):
        hid[h % 2, 16 * (h // 2) : 16 * (h // 2) + 16] = rows[16 * h : 16 * h + 16]
    other = hid[1 - core]
    mine = hid[core]
    loads[1].wait()
    digits, level = encode(dot(other, wkv_ref[...]), 64)
    sx_kv[:, :, :576] = digits.reshape(8, 16, 576)
    sx_kv[:, :, 576:] = level.reshape(8, 16, 64)
    pl.semaphore_wait(barrier, len(greet))
    c_kv = copy(sx_kv, rx_kv, sibling)
    loads[2].wait()
    digits, level = encode(dot(other, wqa_ref[...]), 128)
    sx_q[:, :, :1536] = digits.reshape(8, 16, 1536)
    sx_q[:, :, 1536:] = level.reshape(8, 16, 128)
    c_q = copy(sx_q, rx_q, sibling)
    own_kv[:, :, 576:] = jnp.zeros((8, 16, 64), F32)
    own_kv[:, :, :576] = dot(mine, wkv_ref[...]).reshape(8, 16, 576)
    own_q[...] = dot(mine, wqa_ref[...]).reshape(8, 16, 1536)

    c_kv.wait()
    low = own_kv[:, :, :576] + decode(rx_kv[:, :, :576], rx_kv[:, :, 576:577])
    own_kv[:, :, :576] = low
    digits, level = encode(low.reshape(128, 576), 64)
    st_kv[:, :, :576] = digits.reshape(8, 16, 576)
    st_kv[:, :, 576:] = level.reshape(8, 16, 64)
    p_kv = [copy(st_kv.at[pj], rs_kv.at[i], who) for i, (pj, who) in enumerate(peers)]
    c_q.wait()
    low = own_q[...] + decode(rx_q[:, :, :1536], rx_q[:, :, 1536:1537])
    own_q[...] = low
    digits, level = encode(low.reshape(128, 1536), 128)
    st_q[:, :, :1536] = digits.reshape(8, 16, 1536)
    st_q[:, :, 1536:] = level.reshape(8, 16, 128)
    p_q = [copy(st_q.at[pj], rs_q.at[i], who) for i, (pj, who) in enumerate(peers)]

    h = j * 2 + core
    base = pos_ref[128 * (h // 8)]
    run = base // 128
    tok = (base + (h % 8) * 16 + lax.broadcasted_iota(jnp.int32, (16, 128), 0)).astype(F32)
    lane = lax.broadcasted_iota(jnp.int32, (16, 128), 1)
    angle = tok * inv_row_ref[...]
    cosine, sine = jnp.cos(angle), jnp.sin(angle)
    tail = jnp.where(lane < 96, jnp.where(run > lane - 64, -BIG, 0.0), 0.0)
    loads[3].wait()
    loads[4].wait()
    for i in range(4):
        uk_t[:, 128 * i : 128 * i + 128] = uk_ref[i].T
        up_t[128 * i : 128 * i + 128, :] = up_ref[i].T
    for c in p_kv:
        c.wait()
    low = own_kv[j]
    parts = [decode(rs_kv[i, :, :576], rs_kv[i, :, 576:577]) for i in range(7)]
    latent = low[:, :512] + sum(part[:, :512] for part in parts)
    latent = latent * lax.rsqrt(jnp.mean(latent * latent, -1, keepdims=True) + 1e-06) * kg_ref[...].reshape(1, 512)
    near_ref[core, 0, p, q, :, :512] = latent.astype(BF16)
    rope = sum(part[:, 512:576] for part in parts)
    rope = low[:, 512:] + jnp.concatenate([rope, jnp.zeros((16, 64), F32)], 1)
    swapped = jnp.where(lane < 32, -pltpu.roll(rope, 96, 1), pltpu.roll(rope, 32, 1))
    rope = jnp.where(lane < 64, rope * cosine + swapped * sine, tail)
    near_ref[core, 0, p, q, :, 512:] = rope.astype(BF16)
    block = near_ref.at[core, 0, p, q]
    p_z = [copy(block, far_ref.at[core, p, q, d - 2], zs[d]) for d in range(2, 7)]
    p_p = [copy(block, block, who) for who in plane]

    for c in p_q:
        c.wait()
    low = own_q[j]
    for i in range(7):
        low = low + decode(rs_q[i, :, :1536], rs_q[i, :, 1536:1537])
    low = low * lax.rsqrt(jnp.mean(low * low, -1, keepdims=True) + 1e-06) * qg_ref[...].reshape(1, 1536)
    cq_ref[j, core] = low.astype(BF16)
    block = cq_ref.at[j, core]
    p_c = [copy(block, block, who) for _, who in peers]

    def share(part):
        return copy(part, part, sibling)

    for c in p_p:
        c.wait()
    mine = near_ref.at[core, 0]
    beside = [copy(mine, near_ref.at[core, 1], zs[1]), copy(mine, near_ref.at[core, 2], zs[7])]
    s_near = [share(mine)]

    for c in p_z:
        c.wait()

    def spread(a, steps):
        part = far_ref.at[core, (p + a) % 4, q]
        return [
            copy(part, part, device(
                core, (x + da * (1 - core) + db * core) % 4, (y + da * core + db * (1 - core)) % 4, z,
            ))
            for da, db in steps
        ]

    across = ((0, 1), (0, 3), (0, 2))
    first = spread(0, ((1, 0), (3, 0), (2, 0)))
    lines = {0: spread(0, across)}
    s_lines = {}

    def finish(a):
        for c in lines[a]:
            c.wait()
        s_lines[a] = share(far_ref.at[core, (p + a) % 4])

    sp = y * (1 - core) + x * core
    scale = math.log2(math.e) / math.sqrt(192)

    def near_keys(r, cols):
        return near_ref[:, r, :, :, :, cols].reshape(512, -1)

    def far_keys(a, cols):
        return jnp.concatenate([
            far_ref[core, (p + a) % 4, :, :, :, cols].reshape(320, -1),
            far_ref[1 - core, (sp + a) % 4, :, :, :, cols].reshape(320, -1),
        ], 0)

    def expand(n, keys, which):
        keys = keys(which, slice(0, 512))
        count = keys.shape[0]
        ke[n, :count] = dot(keys, uk_t[...]).astype(BF16)
        vt[n, :, :count] = dot(up_t[...], keys, 1, 1).astype(BF16)

    def attend(n, keys, which, diagonal=False):
        tails = keys(which, slice(512, KW))
        count = tails.shape[0]
        for i in range(4):
            s_ref[i, :count] = dot(jnp.concatenate([ke[n, :count, 128 * i : 128 * i + 128], tails], 1), qt[i])
        if diagonal:
            token = lax.broadcasted_iota(jnp.int32, (16, 256), 1)
            row = lax.broadcasted_iota(jnp.int32, (16, 256), 0)
            for k in range(2):
                for ky in range(4):
                    for half in range(2):
                        at = (ky * 4 + xl + 2 * half) if k else ((xl + 2 * half) * 4 + ky)
                        strip = pl.ds(pl.multiple_of(k * 256 + at * 16, 16), 16)
                        key_token = (ky * 4 + half * 2 + k) * 16 + row
                        hidden = (key_token > token) & (key_token // 128 == token // 128)
                        for i in range(4):
                            s_ref[i, strip] = jnp.where(hidden, -BIG, s_ref[i, strip])
        for i in range(4):
            s = s_ref[i, :count] * scale
            before = m[i]
            now = jnp.maximum(before, jnp.max(s, 0, keepdims=True))
            w = jnp.exp2(s - now)
            fade = jnp.exp2(before - now)
            l[i] = l[i] * fade + jnp.sum(w, 0, keepdims=True)
            m[i] = now
            acc[i] = acc[i] * fade + dot(vt[n, 128 * i : 128 * i + 128, :count], w.astype(BF16))

    m[...] = jnp.full(m.shape, -4 * BIG, F32)
    l[...] = jnp.zeros(l.shape, F32)
    acc[...] = jnp.zeros(acc.shape, F32)
    wide = lax.broadcasted_iota(jnp.int32, (32, 256), 1)
    base = jnp.where(wide < 128, pos_ref[0], pos_ref[128])
    angle = (base + wide % 128).astype(F32) * inv_col_ref[...]
    cosine, sine = jnp.cos(angle), jnp.sin(angle)
    runs = jnp.where(base // 128 == lax.broadcasted_iota(jnp.int32, (32, 256), 0), 1.0, 0.0).astype(BF16)
    s_near[0].wait()
    expand(0, near_keys, 0)
    for c in p_c:
        c.wait()
    mate = cq_ref.at[:, pl.ds(core, 1)]
    c_c = share(mate)
    for c, a in zip(first, (3, 1, 2)):
        c.wait()
        lines[a] = spread(a, across)
    loads[5].wait()
    c_c.wait()
    q_t = dot(cq_ref[...].reshape(256, 1536), wqb_ref[...]).astype(BF16).T
    for i in range(4):
        qt[i, :128] = q_t[192 * i : 192 * i + 128]
        a = q_t[192 * i + 128 : 192 * i + 160].astype(F32)
        b = q_t[192 * i + 160 : 192 * i + 192].astype(F32)
        qt[i, 128:160] = (a * cosine - b * sine).astype(BF16)
        qt[i, 160:192] = (b * cosine + a * sine).astype(BF16)
        qt[i, 192:224] = runs
        qt[i, 224:] = jnp.zeros((32, 256), BF16)
    finish(0)
    attend(0, near_keys, 0, True)
    for r in (1, 2):
        beside[r - 1].wait()
        s_near.append(share(near_ref.at[core, r]))
    s_lines[0].wait()
    expand(3, far_keys, 0)
    finish(3)
    attend(3, far_keys, 0)
    s_near[1].wait()
    expand(1, near_keys, 1)
    attend(1, near_keys, 1)
    finish(1)
    s_lines[3].wait()
    expand(4, far_keys, 3)
    attend(4, far_keys, 3)
    s_near[2].wait()
    expand(2, near_keys, 2)
    attend(2, near_keys, 2)
    finish(2)
    s_lines[1].wait()
    expand(5, far_keys, 1)
    attend(5, far_keys, 1)
    s_lines[2].wait()
    expand(6, far_keys, 2)
    attend(6, far_keys, 2)
    for i in range(4):
        out_ref[:, 128 * i : 128 * i + 128] = (acc[i] / l[i]).T.astype(BF16)


def body(hidden_in, w_qa, w_kva, q_norm_gain, kv_norm_gain, w_qb, w_uk, value_up_weight, positions):
    inverse = 50000.0 ** (-np.arange(0, 64, 2) / 64)
    inv_row = np.zeros((1, 128), np.float32)
    inv_row[0, :32] = inverse
    inv_row[0, 32:64] = inverse
    inv_col = np.repeat(inverse.astype(np.float32)[:, None], 256, 1)
    vmem = pl.BlockSpec(memory_space=pltpu.VMEM)
    smem = pl.BlockSpec(memory_space=pltpu.SMEM)
    any_space = pl.BlockSpec(memory_space=pl.ANY)
    copies = 80
    return pl.pallas_call(
        kernel,
        name="attention",
        out_shape=jax.ShapeDtypeStruct((256, 512), BF16),
        in_specs=[smem] + [vmem] * 4 + [any_space] * 6,
        out_specs=vmem,
        scratch_shapes=[
            pltpu.VMEM((448, 256), BF16), pltpu.VMEM((448, 1536), BF16), pltpu.VMEM((448, 576), BF16),
            pltpu.VMEM((1536, 768), BF16), pltpu.VMEM((4, 128, 512), BF16), pltpu.VMEM((4, 512, 128), BF16),
            pltpu.VMEM((2, 128, 448), BF16), pltpu.VMEM((512, 512), BF16), pltpu.VMEM((512, 512), BF16),
            pltpu.VMEM((8, 16, KW), I16), pltpu.VMEM((8, 16, KW), I16),
            pltpu.VMEM((8, 16, QW), I16), pltpu.VMEM((8, 16, QW), I16),
            pltpu.VMEM((8, 16, KW), F32), pltpu.VMEM((8, 16, 1536), F32),
            pltpu.VMEM((8, 16, KW), I16), pltpu.VMEM((8, 16, QW), I16),
            pltpu.VMEM((7, 16, KW), I16), pltpu.VMEM((7, 16, QW), I16),
            pltpu.VMEM((8, 2, 16, 1536), BF16), pltpu.VMEM((2, 3, 4, 4, 16, KW), BF16),
            pltpu.VMEM((2, 4, 4, 5, 16, KW), BF16),
            pltpu.VMEM((7, 640, 512), BF16), pltpu.VMEM((7, 512, 640), BF16),
            pltpu.VMEM((4, 256, 256), BF16), pltpu.VMEM((4, 640, 256), F32),
            pltpu.VMEM((4, 128, 256), F32), pltpu.VMEM((4, 1, 256), F32), pltpu.VMEM((4, 1, 256), F32),
            pltpu.SemaphoreType.DMA((copies,)), pltpu.SemaphoreType.DMA((copies,)), pltpu.SemaphoreType.DMA((6,)),
        ],
        compiler_params=pltpu.CompilerParams(
            collective_id=0, has_side_effects=True, vmem_limit_bytes=60 * 2**20
        ),
    )(
        positions, jnp.asarray(inv_row), jnp.asarray(inv_col), q_norm_gain, kv_norm_gain,
        hidden_in.T, w_qa, w_kva, w_qb, w_uk, value_up_weight,
    )


def solution(mesh):
    return jax.shard_map(
        body,
        mesh=mesh,
        in_specs=(
            P("seq", "head"), P("head", None), P("head", None), P(), P(), P(None, "head"),
            P("head", None, None), P("head", None, None), P("seq"),
        ),
        out_specs=P("seq", "head"),
        check_vma=False,
    )
```

```python
import functools
import math

import jax
import jax.numpy as jnp
import numpy as np
from jax import lax
from jax.experimental import pallas as pl
from jax.experimental.pallas import tpu as pltpu
from jax.sharding import PartitionSpec as P

MESH = pl.DeviceIdType.MESH
F32 = jnp.float32
BF16 = jnp.bfloat16
I16 = jnp.int16
BIG = 2.0**100
KW = 640
QW = 1536 + 128


def place():
    s = lax.axis_index("seq")
    h = lax.axis_index("head")
    return h % 2, ((h // 2) % 2) * 2 + s // 8, h // 4, s % 8


def device(core, x, y, z):
    return ((x % 2) * 8 + z, y * 4 + (x // 2) * 2 + core)


def dot(a, b, over_a=1, over_b=0):
    return lax.dot_general(a, b, (((over_a,), (over_b,)), ((), ())), preferred_element_type=F32)


def encode(values, width):
    rows = values.shape[0]
    top = jnp.maximum(jnp.max(jnp.abs(values), -1, keepdims=True), 2.0**-60)
    level = jnp.ceil(jnp.log2(top) * 512.0)
    digits = jnp.round(values * (jnp.exp2(level * (-1.0 / 512.0)) * 32700.0))
    return digits.astype(jnp.int32).astype(I16), jnp.broadcast_to(level, (rows, width)).astype(jnp.int32).astype(I16)


def decode(digits, level):
    unit = jnp.exp2(level.astype(jnp.int32).astype(F32) * (1.0 / 512.0)) * (1.0 / 32700.0)
    return digits.astype(jnp.int32).astype(F32) * unit


def kernel(
    pos_ref, row_hbm, col_hbm, qg_hbm, kg_hbm, hid_hbm, wqa_hbm, wkv_hbm, wqb_hbm, uk_hbm, up_hbm,
    out_ref,
    inv_row_ref, inv_col_ref, qg_ref, kg_ref, hid_t, wqa_ref, wkv_ref, wqb_ref, uk_ref, up_ref, hid, uk_t, up_t,
    sx_kv, rx_kv, sx_q, rx_q, own_kv, own_q, st_kv, st_q, rs_kv, rs_q,
    cq_ref, near_ref, far_ref, ke, vt, qt, s_ref, acc, m, l,
    send, recv, load,
):
    core, x, y, z = place()
    xh, xl = x // 2, x % 2
    j = y * 2 + xh
    p = x * (1 - core) + y * core
    q = y * (1 - core) + x * core
    used = [0]

    loads = []

    def fetch(*pairs):
        for src, dst in pairs:
            loads.append(pltpu.make_async_copy(src, dst, load.at[len(loads)]))
            loads[-1].start()

    fetch((hid_hbm, hid_t), (wkv_hbm, wkv_ref))

    def copy(src, dst, target):
        at = used[0]
        used[0] += 1
        done = pltpu.make_async_remote_copy(
            src_ref=src, dst_ref=dst, send_sem=send.at[at], recv_sem=recv.at[at],
            device_id=target, device_id_type=MESH,
        )
        done.start()
        return done

    sibling = device(1 - core, x, y, z)
    peers = []
    for dy, dx in ((2, 1), (1, 1), (3, 1), (2, 0), (0, 1), (1, 0), (3, 0)):
        py, px = (y + dy) % 4, (xh + dx) % 2
        peers.append((py * 2 + px, device(core, px * 2 + xl, py, z)))
    zs = [device(core, x, y, (z + d) % 8) for d in range(8)]
    order = (10, 9, 11, 6, 14, 2, 8, 5, 7, 13, 15, 1, 3, 4, 12)
    plane = [device(core, (x + d % 4) % 4, (y + d // 4) % 4, z) for d in order]
    barrier = pltpu.get_barrier_semaphore()
    greet = [sibling] + zs[1:] + plane
    for who in greet:
        pl.semaphore_signal(barrier, inc=1, device_id=who, device_id_type=MESH)

    loads[0].wait()
    rows = hid_t[...].T
    for h in range(16):
        hid[h % 2, 16 * (h // 2) : 16 * (h // 2) + 16] = rows[16 * h : 16 * h + 16]
    other = hid[1 - core]
    mine = hid[core]
    loads[1].wait()
    fetch((wqa_hbm, wqa_ref))
    digits, level = encode(dot(other, wkv_ref[...]), 64)
    sx_kv[:, :, :576] = digits.reshape(8, 16, 576)
    sx_kv[:, :, 576:] = level.reshape(8, 16, 64)
    pl.semaphore_wait(barrier, len(greet))
    c_kv = copy(sx_kv, rx_kv, sibling)
    loads[2].wait()
    digits, level = encode(dot(other, wqa_ref[...]), 128)
    sx_q[:, :, :1536] = digits.reshape(8, 16, 1536)
    sx_q[:, :, 1536:] = level.reshape(8, 16, 128)
    c_q = copy(sx_q, rx_q, sibling)
    fetch((uk_hbm, uk_ref), (up_hbm, up_ref), (qg_hbm, qg_ref), (kg_hbm, kg_ref), (row_hbm, inv_row_ref), (col_hbm, inv_col_ref))
    low = dot(mine, wkv_ref[...]).reshape(8, 16, 576)

    c_kv.wait()
    low = low + decode(rx_kv[:, :, :576], rx_kv[:, :, 576:577])
    own_kv[:, :, :576] = low
    own_kv[:, :, 576:] = jnp.zeros((8, 16, 64), F32)
    digits, level = encode(low.reshape(128, 576), 64)
    st_kv[:, :, :576] = digits.reshape(8, 16, 576)
    st_kv[:, :, 576:] = level.reshape(8, 16, 64)
    p_kv = [copy(st_kv.at[pj], rs_kv.at[i], who) for i, (pj, who) in enumerate(peers)]
    low = dot(mine, wqa_ref[...]).reshape(8, 16, 1536)
    c_q.wait()
    low = low + decode(rx_q[:, :, :1536], rx_q[:, :, 1536:1537])
    own_q[...] = low
    digits, level = encode(low.reshape(128, 1536), 128)
    st_q[:, :, :1536] = digits.reshape(8, 16, 1536)
    st_q[:, :, 1536:] = level.reshape(8, 16, 128)
    p_q = [copy(st_q.at[pj], rs_q.at[i], who) for i, (pj, who) in enumerate(peers)]

    fetch((wqb_hbm, wqb_ref))

    h = j * 2 + core
    base = pos_ref[128 * (h // 8)]
    run = base // 128
    tok = (base + (h % 8) * 16 + lax.broadcasted_iota(jnp.int32, (16, 128), 0)).astype(F32)
    lane = lax.broadcasted_iota(jnp.int32, (16, 128), 1)
    for i in range(3, 9):
        loads[i].wait()
    angle = tok * inv_row_ref[...]
    cosine, sine = jnp.cos(angle), jnp.sin(angle)
    tail = jnp.where(lane < 96, jnp.where(run > lane - 64, -BIG, 0.0), 0.0)
    for i in range(4):
        uk_t[:, 128 * i : 128 * i + 128] = uk_ref[i].T
        up_t[128 * i : 128 * i + 128, :] = up_ref[i].T
    for c in p_kv:
        c.wait()
    low = own_kv[j]
    parts = [decode(rs_kv[i, :, :576], rs_kv[i, :, 576:577]) for i in range(7)]
    latent = low[:, :512] + sum(part[:, :512] for part in parts)
    latent = latent * lax.rsqrt(jnp.mean(latent * latent, -1, keepdims=True) + 1e-06) * kg_ref[...].reshape(1, 512)
    near_ref[core, 0, p, q, :, :512] = latent.astype(BF16)
    rope = sum(part[:, 512:576] for part in parts)
    rope = low[:, 512:] + jnp.concatenate([rope, jnp.zeros((16, 64), F32)], 1)
    swapped = jnp.where(lane < 32, -pltpu.roll(rope, 96, 1), pltpu.roll(rope, 32, 1))
    rope = jnp.where(lane < 64, rope * cosine + swapped * sine, tail)
    near_ref[core, 0, p, q, :, 512:] = rope.astype(BF16)
    block = near_ref.at[core, 0, p, q]
    p_z = [copy(block, far_ref.at[core, p, q, d - 2], zs[d]) for d in (2, 6, 3, 5, 4)]
    p_p = [copy(block, block, who) for who in plane]

    for c in p_q:
        c.wait()
    low = own_q[j]
    for i in range(7):
        low = low + decode(rs_q[i, :, :1536], rs_q[i, :, 1536:1537])
    low = low * lax.rsqrt(jnp.mean(low * low, -1, keepdims=True) + 1e-06) * qg_ref[...].reshape(1, 1536)
    cq_ref[j, core] = low.astype(BF16)
    block = cq_ref.at[j, core]
    p_c = [copy(block, block, who) for _, who in peers]

    def share(part):
        return copy(part, part, sibling)

    for c in p_z:
        c.wait()

    def spread(a, steps):
        part = far_ref.at[core, (p + a) % 4, q]
        return [
            copy(part, part, device(
                core, (x + da * (1 - core) + db * core) % 4, (y + da * core + db * (1 - core)) % 4, z,
            ))
            for da, db in steps
        ]

    across = ((0, 1), (0, 3), (0, 2))
    first = spread(0, ((1, 0), (3, 0), (2, 0)))
    lines = {0: spread(0, across)}
    s_lines = {}

    for c in p_p:
        c.wait()
    mine = near_ref.at[core, 0]
    beside = [copy(mine, near_ref.at[core, 1], zs[1]), copy(mine, near_ref.at[core, 2], zs[7])]
    s_near = [share(mine)]

    def finish(a):
        for c in lines[a]:
            c.wait()
        s_lines[a] = share(far_ref.at[core, (p + a) % 4])

    sp = y * (1 - core) + x * core
    scale = math.log2(math.e) / math.sqrt(192)

    def near_keys(r, cols):
        return near_ref[:, r, :, :, :, cols].reshape(512, -1)

    def far_keys(a, cols):
        return jnp.concatenate([
            far_ref[core, (p + a) % 4, :, :, :, cols].reshape(320, -1),
            far_ref[1 - core, (sp + a) % 4, :, :, :, cols].reshape(320, -1),
        ], 0)

    def expand(n, keys, which):
        keys = keys(which, slice(0, 512))
        count = keys.shape[0]
        ke[n, :count] = (dot(keys, uk_t[...]) * scale).astype(BF16)
        vt[n, :, :count] = dot(up_t[...], keys, 1, 1).astype(BF16)

    def score(n, keys, which, i, diagonal=False):
        tails = keys(which, slice(512, KW))
        count = tails.shape[0]
        s_ref[n % 2, i, :count] = dot(jnp.concatenate([ke[n, :count, 128 * i : 128 * i + 128], tails], 1), qt[i])
        if diagonal:
            at = lax.broadcasted_iota(jnp.int32, (16, 256), 1)
            token = at % 128 // 16 * 32 + at // 128 * 16 + at % 16
            row = lax.broadcasted_iota(jnp.int32, (16, 256), 0)
            for k in range(2):
                for ky in range(4):
                    for half in range(2):
                        at = (ky * 4 + xl + 2 * half) if k else ((xl + 2 * half) * 4 + ky)
                        strip = pl.ds(pl.multiple_of(k * 256 + at * 16, 16), 16)
                        key_token = (ky * 4 + half * 2 + k) * 16 + row
                        hidden = (key_token > token) & (key_token // 128 == token // 128)
                        s_ref[n % 2, i, strip] = jnp.where(hidden, -BIG, s_ref[n % 2, i, strip])

    def weigh(n, count, i):
        s = s_ref[n % 2, i, :count]
        before = m[i]
        now = jnp.maximum(before, jnp.max(s, 0, keepdims=True))
        w = jnp.exp2(s - now)
        fade = jnp.exp2(before - now)
        l[i] = l[i] * fade + jnp.sum(w, 0, keepdims=True)
        m[i] = now
        acc[i] = acc[i] * fade + dot(vt[n, 128 * i : 128 * i + 128, :count], w.astype(BF16))

    def step(n, count, keys, which):
        for i in range(4):
            score(n, keys, which, i)
            weigh(n - 1, count, i)

    m[...] = jnp.full(m.shape, -4 * BIG, F32)
    l[...] = jnp.zeros(l.shape, F32)
    acc[...] = jnp.zeros(acc.shape, F32)

    def queries(k):
        wide = lax.broadcasted_iota(jnp.int32, (32, 128), 1)
        base = jnp.where(wide < 64, pos_ref[0], pos_ref[128])
        angle = (base + wide % 64 // 16 * 32 + k * 16 + wide % 16).astype(F32) * inv_col_ref[...]
        cosine, sine = jnp.cos(angle), jnp.sin(angle)
        runs = jnp.where(base // 128 == lax.broadcasted_iota(jnp.int32, (32, 128), 0), 1.0, 0.0).astype(BF16)
        at = pl.ds(pl.multiple_of(k * 128, 128), 128)
        q_t = dot(cq_ref[:, pl.ds(k, 1)].reshape(128, 1536), wqb_ref[...]).astype(BF16).T
        for i in range(4):
            qt[i, :128, at] = q_t[192 * i : 192 * i + 128]
            a = q_t[192 * i + 128 : 192 * i + 160].astype(F32)
            b = q_t[192 * i + 160 : 192 * i + 192].astype(F32)
            qt[i, 128:160, at] = ((a * cosine - b * sine) * scale).astype(BF16)
            qt[i, 160:192, at] = ((b * cosine + a * sine) * scale).astype(BF16)
            qt[i, 192:224, at] = runs
            qt[i, 224:, at] = jnp.zeros((32, 128), BF16)

    s_near[0].wait()
    expand(0, near_keys, 0)
    for c in p_c:
        c.wait()
    mate = cq_ref.at[:, pl.ds(core, 1)]
    c_c = share(mate)
    for n, a in ((0, 3), (1, 1), (2, 2)):
        first[n].wait()
        lines[a] = spread(a, across)
    loads[9].wait()
    queries(core)
    c_c.wait()
    queries(1 - core)
    finish(0)
    for i in range(4):
        score(0, near_keys, 0, i, True)
    for r in (1, 2):
        beside[r - 1].wait()
        s_near.append(share(near_ref.at[core, r]))
    s_lines[0].wait()
    expand(1, far_keys, 0)
    step(1, 512, far_keys, 0)
    finish(3)
    s_near[1].wait()
    expand(2, near_keys, 1)
    step(2, 640, near_keys, 1)
    s_near[2].wait()
    expand(3, near_keys, 2)
    step(3, 512, near_keys, 2)
    finish(1)
    s_lines[3].wait()
    expand(4, far_keys, 3)
    step(4, 512, far_keys, 3)
    s_lines[1].wait()
    expand(5, far_keys, 1)
    finish(2)
    step(5, 640, far_keys, 1)
    s_lines[2].wait()
    expand(6, far_keys, 2)
    step(6, 640, far_keys, 2)
    for i in range(4):
        weigh(6, 640, i)
    for i in range(4):
        values = (acc[i] / l[i]).T.astype(BF16)
        for k in range(2):
            out_ref[:, k, :, 128 * i : 128 * i + 128] = values[128 * k : 128 * k + 128].reshape(8, 16, 128)


def body(hidden_in, w_qa, w_kva, q_norm_gain, kv_norm_gain, w_qb, w_uk, value_up_weight, positions):
    inverse = 50000.0 ** (-np.arange(0, 64, 2) / 64)
    inv_row = np.zeros((1, 128), np.float32)
    inv_row[0, :32] = inverse
    inv_row[0, 32:64] = inverse
    inv_col = np.repeat(inverse.astype(np.float32)[:, None], 128, 1)
    vmem = pl.BlockSpec(memory_space=pltpu.VMEM)
    smem = pl.BlockSpec(memory_space=pltpu.SMEM)
    any_space = pl.BlockSpec(memory_space=pl.ANY)
    copies = 80
    return pl.pallas_call(
        kernel,
        name="attention",
        out_shape=jax.ShapeDtypeStruct((8, 2, 16, 512), BF16),
        in_specs=[smem] + [any_space] * 10,
        out_specs=vmem,
        scratch_shapes=[
            pltpu.VMEM((1, 128), F32), pltpu.VMEM((32, 128), F32), pltpu.VMEM((1536,), F32), pltpu.VMEM((512,), F32),
            pltpu.VMEM((448, 256), BF16), pltpu.VMEM((448, 1536), BF16), pltpu.VMEM((448, 576), BF16),
            pltpu.VMEM((1536, 768), BF16), pltpu.VMEM((4, 128, 512), BF16), pltpu.VMEM((4, 512, 128), BF16),
            pltpu.VMEM((2, 128, 448), BF16), pltpu.VMEM((512, 512), BF16), pltpu.VMEM((512, 512), BF16),
            pltpu.VMEM((8, 16, KW), I16), pltpu.VMEM((8, 16, KW), I16),
            pltpu.VMEM((8, 16, QW), I16), pltpu.VMEM((8, 16, QW), I16),
            pltpu.VMEM((8, 16, KW), F32), pltpu.VMEM((8, 16, 1536), F32),
            pltpu.VMEM((8, 16, KW), I16), pltpu.VMEM((8, 16, QW), I16),
            pltpu.VMEM((7, 16, KW), I16), pltpu.VMEM((7, 16, QW), I16),
            pltpu.VMEM((8, 2, 16, 1536), BF16), pltpu.VMEM((2, 3, 4, 4, 16, KW), BF16),
            pltpu.VMEM((2, 4, 4, 5, 16, KW), BF16),
            pltpu.VMEM((7, 640, 512), BF16), pltpu.VMEM((7, 512, 640), BF16),
            pltpu.VMEM((4, 256, 256), BF16), pltpu.VMEM((2, 4, 640, 256), F32),
            pltpu.VMEM((4, 128, 256), F32), pltpu.VMEM((4, 1, 256), F32), pltpu.VMEM((4, 1, 256), F32),
            pltpu.SemaphoreType.DMA((copies,)), pltpu.SemaphoreType.DMA((copies,)), pltpu.SemaphoreType.DMA((10,)),
        ],
        compiler_params=pltpu.CompilerParams(
            collective_id=0, has_side_effects=True, vmem_limit_bytes=60 * 2**20
        ),
    )(
        positions, jnp.asarray(inv_row), jnp.asarray(inv_col), q_norm_gain, kv_norm_gain,
        hidden_in.T, w_qa, w_kva, w_qb, w_uk, value_up_weight,
    ).reshape(256, 512)


def solution(mesh):
    return jax.shard_map(
        body,
        mesh=mesh,
        in_specs=(
            P("seq", "head"), P("head", None), P("head", None), P(), P(), P(None, "head"),
            P("head", None, None), P("head", None, None), P("seq"),
        ),
        out_specs=P("seq", "head"),
        check_vma=False,
    )
```

```python
import functools
import math

import jax
import jax.numpy as jnp
import numpy as np
from jax import lax
from jax.experimental import pallas as pl
from jax.experimental.pallas import tpu as pltpu
from jax.sharding import PartitionSpec as P

MESH = pl.DeviceIdType.MESH
F32 = jnp.float32
BF16 = jnp.bfloat16
I16 = jnp.int16
BIG = 2.0**100
KW = 640
QW = 1536 + 128


def place():
    s = lax.axis_index("seq")
    h = lax.axis_index("head")
    return h % 2, ((h // 2) % 2) * 2 + s // 8, h // 4, s % 8


def device(core, x, y, z):
    return ((x % 2) * 8 + z, y * 4 + (x // 2) * 2 + core)


def dot(a, b, over_a=1, over_b=0):
    return lax.dot_general(a, b, (((over_a,), (over_b,)), ((), ())), preferred_element_type=F32)


def encode(values, width):
    rows = values.shape[0]
    top = jnp.maximum(jnp.max(jnp.abs(values), -1, keepdims=True), 2.0**-60)
    level = jnp.ceil(jnp.log2(top) * 512.0)
    digits = jnp.round(values * (jnp.exp2(level * (-1.0 / 512.0)) * 32700.0))
    return digits.astype(jnp.int32).astype(I16), jnp.broadcast_to(level, (rows, width)).astype(jnp.int32).astype(I16)


def decode(digits, level):
    unit = jnp.exp2(level.astype(jnp.int32).astype(F32) * (1.0 / 512.0)) * (1.0 / 32700.0)
    return digits.astype(jnp.int32).astype(F32) * unit


def kernel(
    pos_ref, row_hbm, col_hbm, qg_hbm, kg_hbm, hid_hbm, wqa_hbm, wkv_hbm, wqb_hbm, uk_hbm, up_hbm,
    out_ref,
    inv_row_ref, inv_col_ref, qg_ref, kg_ref, hid_t, wqa_ref, wkv_ref, wqb_ref, uk_ref, up_ref, hid, uk_t, up_t,
    sx_kv, rx_kv, sx_q, rx_q, own_kv, own_q, st_kv, st_q, rs_kv, rs_q,
    cq_ref, near_ref, far_ref, ke, vt, qt, s_ref, acc, m, l,
    send, recv, load,
):
    core, x, y, z = place()
    xh, xl = x // 2, x % 2
    j = y * 2 + xh
    p = x * (1 - core) + y * core
    q = y * (1 - core) + x * core
    used = [0]

    loads = []

    def fetch(*pairs):
        for src, dst in pairs:
            loads.append(pltpu.make_async_copy(src, dst, load.at[len(loads)]))
            loads[-1].start()

    fetch((hid_hbm, hid_t), (wkv_hbm, wkv_ref))

    def copy(src, dst, target):
        at = used[0]
        used[0] += 1
        done = pltpu.make_async_remote_copy(
            src_ref=src, dst_ref=dst, send_sem=send.at[at], recv_sem=recv.at[at],
            device_id=target, device_id_type=MESH,
        )
        done.start()
        return done

    sibling = device(1 - core, x, y, z)
    peers = []
    for dy, dx in ((2, 1), (1, 1), (3, 1), (2, 0), (0, 1), (1, 0), (3, 0)):
        py, px = (y + dy) % 4, (xh + dx) % 2
        peers.append((py * 2 + px, device(core, px * 2 + xl, py, z)))
    zs = [device(core, x, y, (z + d) % 8) for d in range(8)]
    order = (10, 9, 11, 6, 14, 2, 8, 5, 7, 13, 15, 1, 3, 4, 12)
    plane = [device(core, (x + d % 4) % 4, (y + d // 4) % 4, z) for d in order]
    barrier = pltpu.get_barrier_semaphore()
    greet = [sibling] + zs[1:] + plane
    for who in greet:
        pl.semaphore_signal(barrier, inc=1, device_id=who, device_id_type=MESH)

    loads[0].wait()
    rows = hid_t[...].T
    for h in range(16):
        hid[h % 2, 16 * (h // 2) : 16 * (h // 2) + 16] = rows[16 * h : 16 * h + 16]
    other = hid[1 - core]
    mine = hid[core]
    loads[1].wait()
    fetch((wqa_hbm, wqa_ref))
    digits, level = encode(dot(other, wkv_ref[...]), 64)
    sx_kv[:, :, :576] = digits.reshape(8, 16, 576)
    sx_kv[:, :, 576:] = level.reshape(8, 16, 64)
    pl.semaphore_wait(barrier, len(greet))
    c_kv = copy(sx_kv, rx_kv, sibling)
    loads[2].wait()
    digits, level = encode(dot(other, wqa_ref[...]), 128)
    sx_q[:, :, :1536] = digits.reshape(8, 16, 1536)
    sx_q[:, :, 1536:] = level.reshape(8, 16, 128)
    c_q = copy(sx_q, rx_q, sibling)
    fetch((uk_hbm, uk_ref), (up_hbm, up_ref), (qg_hbm, qg_ref), (kg_hbm, kg_ref), (row_hbm, inv_row_ref), (col_hbm, inv_col_ref))
    low = dot(mine, wkv_ref[...]).reshape(8, 16, 576)

    c_kv.wait()
    low = low + decode(rx_kv[:, :, :576], rx_kv[:, :, 576:577])
    own_kv[:, :, :576] = low
    own_kv[:, :, 576:] = jnp.zeros((8, 16, 64), F32)
    digits, level = encode(low.reshape(128, 576), 64)
    st_kv[:, :, :576] = digits.reshape(8, 16, 576)
    st_kv[:, :, 576:] = level.reshape(8, 16, 64)
    p_kv = [copy(st_kv.at[pj], rs_kv.at[i], who) for i, (pj, who) in enumerate(peers)]
    low = dot(mine, wqa_ref[...]).reshape(8, 16, 1536)
    c_q.wait()
    low = low + decode(rx_q[:, :, :1536], rx_q[:, :, 1536:1537])
    own_q[...] = low
    digits, level = encode(low.reshape(128, 1536), 128)
    st_q[:, :, :1536] = digits.reshape(8, 16, 1536)
    st_q[:, :, 1536:] = level.reshape(8, 16, 128)
    p_q = [copy(st_q.at[pj], rs_q.at[i], who) for i, (pj, who) in enumerate(peers)]

    fetch((wqb_hbm, wqb_ref))

    h = j * 2 + core
    base = pos_ref[128 * (h // 8)]
    run = base // 128
    tok = (base + (h % 8) * 16 + lax.broadcasted_iota(jnp.int32, (16, 128), 0)).astype(F32)
    lane = lax.broadcasted_iota(jnp.int32, (16, 128), 1)
    for i in range(3, 9):
        loads[i].wait()
    angle = tok * inv_row_ref[...]
    cosine, sine = jnp.cos(angle), jnp.sin(angle)
    tail = jnp.where(lane < 96, jnp.where(run > lane - 64, -BIG, 0.0), 0.0)
    for i in range(4):
        uk_t[:, 128 * i : 128 * i + 128] = uk_ref[i].T
        up_t[128 * i : 128 * i + 128, :] = up_ref[i].T
    for c in p_kv:
        c.wait()
    low = own_kv[j]
    parts = [decode(rs_kv[i, :, :576], rs_kv[i, :, 576:577]) for i in range(7)]
    latent = low[:, :512] + sum(part[:, :512] for part in parts)
    latent = latent * lax.rsqrt(jnp.mean(latent * latent, -1, keepdims=True) + 1e-06) * kg_ref[...].reshape(1, 512)
    near_ref[core, 0, p, q, :, :512] = latent.astype(BF16)
    rope = sum(part[:, 512:576] for part in parts)
    rope = low[:, 512:] + jnp.concatenate([rope, jnp.zeros((16, 64), F32)], 1)
    swapped = jnp.where(lane < 32, -pltpu.roll(rope, 96, 1), pltpu.roll(rope, 32, 1))
    rope = jnp.where(lane < 64, rope * cosine + swapped * sine, tail)
    near_ref[core, 0, p, q, :, 512:] = rope.astype(BF16)
    block = near_ref.at[core, 0, p, q]
    p_z = [copy(block, far_ref.at[core, p, q, d - 2], zs[d]) for d in (2, 6, 3, 5, 4)]
    p_p = [copy(block, block, who) for who in plane]

    for c in p_q:
        c.wait()
    low = own_q[j]
    for i in range(7):
        low = low + decode(rs_q[i, :, :1536], rs_q[i, :, 1536:1537])
    low = low * lax.rsqrt(jnp.mean(low * low, -1, keepdims=True) + 1e-06) * qg_ref[...].reshape(1, 1536)
    cq_ref[j, core] = low.astype(BF16)
    block = cq_ref.at[j, core]
    p_c = [copy(block, block, who) for _, who in peers]

    def share(part):
        return copy(part, part, sibling)

    for c in p_z:
        c.wait()

    def spread(a, steps):
        part = far_ref.at[core, (p + a) % 4, q]
        return [
            copy(part, part, device(
                core, (x + da * (1 - core) + db * core) % 4, (y + da * core + db * (1 - core)) % 4, z,
            ))
            for da, db in steps
        ]

    across = ((0, 1), (0, 3), (0, 2))
    first = spread(0, ((1, 0), (3, 0), (2, 0)))
    lines = {0: spread(0, across)}
    s_lines = {}

    for c in p_p:
        c.wait()
    mine = near_ref.at[core, 0]
    beside = [copy(mine, near_ref.at[core, 1], zs[1]), copy(mine, near_ref.at[core, 2], zs[7])]
    s_near = [share(mine)]

    def finish(a):
        for c in lines[a]:
            c.wait()
        s_lines[a] = share(far_ref.at[core, (p + a) % 4])

    sp = y * (1 - core) + x * core
    scale = math.log2(math.e) / math.sqrt(192)

    def near_keys(r, cols):
        return near_ref[:, r, :, :, :, cols].reshape(512, -1)

    def far_keys(a, cols):
        return jnp.concatenate([
            far_ref[core, (p + a) % 4, :, :, :, cols].reshape(320, -1),
            far_ref[1 - core, (sp + a) % 4, :, :, :, cols].reshape(320, -1),
        ], 0)

    def expand(n, keys, which):
        keys = keys(which, slice(0, 512))
        count = keys.shape[0]
        ke[n, :count] = (dot(keys, uk_t[...]) * scale).astype(BF16)
        vt[n, :, :count] = dot(up_t[...], keys, 1, 1).astype(BF16)

    def score(n, keys, which, i, diagonal=False):
        tails = keys(which, slice(512, KW))
        count = tails.shape[0]
        s_ref[n % 2, i, :count] = dot(jnp.concatenate([ke[n, :count, 128 * i : 128 * i + 128], tails], 1), qt[i])
        if diagonal:
            at = lax.broadcasted_iota(jnp.int32, (16, 256), 1)
            token = at % 128 // 16 * 32 + at // 128 * 16 + at % 16
            row = lax.broadcasted_iota(jnp.int32, (16, 256), 0)
            for k in range(2):
                for ky in range(4):
                    for half in range(2):
                        at = (ky * 4 + xl + 2 * half) if k else ((xl + 2 * half) * 4 + ky)
                        strip = pl.ds(pl.multiple_of(k * 256 + at * 16, 16), 16)
                        key_token = (ky * 4 + half * 2 + k) * 16 + row
                        hidden = (key_token > token) & (key_token // 128 == token // 128)
                        s_ref[n % 2, i, strip] = jnp.where(hidden, -BIG, s_ref[n % 2, i, strip])

    def weigh(n, count, i):
        s = s_ref[n % 2, i, :count]
        before = m[i]
        now = jnp.maximum(before, jnp.max(s, 0, keepdims=True))
        w = jnp.exp2(s - now)
        fade = jnp.exp2(before - now)
        l[i] = l[i] * fade + jnp.sum(w, 0, keepdims=True)
        m[i] = now
        acc[i] = acc[i] * fade + dot(vt[n, 128 * i : 128 * i + 128, :count], w.astype(BF16))

    def step(n, count, keys, which):
        for i in range(4):
            score(n, keys, which, i)
            weigh(n - 1, count, i)

    m[...] = jnp.full(m.shape, -4 * BIG, F32)
    l[...] = jnp.zeros(l.shape, F32)
    acc[...] = jnp.zeros(acc.shape, F32)

    def queries(k):
        wide = lax.broadcasted_iota(jnp.int32, (32, 128), 1)
        base = jnp.where(wide < 64, pos_ref[0], pos_ref[128])
        angle = (base + wide % 64 // 16 * 32 + k * 16 + wide % 16).astype(F32) * inv_col_ref[...]
        cosine, sine = jnp.cos(angle), jnp.sin(angle)
        runs = jnp.where(base // 128 == lax.broadcasted_iota(jnp.int32, (32, 128), 0), 1.0, 0.0).astype(BF16)
        at = pl.ds(pl.multiple_of(k * 128, 128), 128)
        q_t = dot(cq_ref[:, pl.ds(k, 1)].reshape(128, 1536), wqb_ref[...]).astype(BF16).T
        for i in range(4):
            qt[i, :128, at] = q_t[192 * i : 192 * i + 128]
            a = q_t[192 * i + 128 : 192 * i + 160].astype(F32)
            b = q_t[192 * i + 160 : 192 * i + 192].astype(F32)
            qt[i, 128:160, at] = ((a * cosine - b * sine) * scale).astype(BF16)
            qt[i, 160:192, at] = ((b * cosine + a * sine) * scale).astype(BF16)
            qt[i, 192:224, at] = runs
            qt[i, 224:, at] = jnp.zeros((32, 128), BF16)

    s_near[0].wait()
    expand(0, near_keys, 0)
    for c in p_c:
        c.wait()
    mate = cq_ref.at[:, pl.ds(core, 1)]
    c_c = share(mate)
    for n, a in ((0, 3), (1, 1), (2, 2)):
        first[n].wait()
        lines[a] = spread(a, across)
    loads[9].wait()
    queries(core)
    c_c.wait()
    queries(1 - core)
    finish(0)
    for i in range(4):
        score(0, near_keys, 0, i, True)
    for r in (1, 2):
        beside[r - 1].wait()
        s_near.append(share(near_ref.at[core, r]))
    s_lines[0].wait()
    expand(1, far_keys, 0)
    step(1, 512, far_keys, 0)
    finish(3)
    s_near[1].wait()
    expand(2, near_keys, 1)
    step(2, 640, near_keys, 1)
    s_near[2].wait()
    expand(3, near_keys, 2)
    step(3, 512, near_keys, 2)
    finish(1)
    s_lines[3].wait()
    expand(4, far_keys, 3)
    step(4, 512, far_keys, 3)
    s_lines[1].wait()
    expand(5, far_keys, 1)
    finish(2)
    step(5, 640, far_keys, 1)
    s_lines[2].wait()
    expand(6, far_keys, 2)
    step(6, 640, far_keys, 2)
    for i in range(4):
        weigh(6, 640, i)
    for i in range(4):
        values = (acc[i] / l[i]).T.astype(BF16)
        for k in range(2):
            out_ref[:, k, :, 128 * i : 128 * i + 128] = values[128 * k : 128 * k + 128].reshape(8, 16, 128)


def body(hidden_in, w_qa, w_kva, q_norm_gain, kv_norm_gain, w_qb, w_uk, value_up_weight, positions):
    inverse = 50000.0 ** (-np.arange(0, 64, 2) / 64)
    inv_row = np.zeros((1, 128), np.float32)
    inv_row[0, :32] = inverse
    inv_row[0, 32:64] = inverse
    inv_col = np.repeat(inverse.astype(np.float32)[:, None], 128, 1)
    vmem = pl.BlockSpec(memory_space=pltpu.VMEM)
    smem = pl.BlockSpec(memory_space=pltpu.SMEM)
    any_space = pl.BlockSpec(memory_space=pl.ANY)
    copies = 80
    return pl.pallas_call(
        kernel,
        name="attention",
        out_shape=pltpu.VMEM((8, 2, 16, 512), BF16),
        in_specs=[smem] + [any_space] * 10,
        out_specs=vmem,
        scratch_shapes=[
            pltpu.VMEM((1, 128), F32), pltpu.VMEM((32, 128), F32), pltpu.VMEM((1536,), F32), pltpu.VMEM((512,), F32),
            pltpu.VMEM((448, 256), BF16), pltpu.VMEM((448, 1536), BF16), pltpu.VMEM((448, 576), BF16),
            pltpu.VMEM((1536, 768), BF16), pltpu.VMEM((4, 128, 512), BF16), pltpu.VMEM((4, 512, 128), BF16),
            pltpu.VMEM((2, 128, 448), BF16), pltpu.VMEM((512, 512), BF16), pltpu.VMEM((512, 512), BF16),
            pltpu.VMEM((8, 16, KW), I16), pltpu.VMEM((8, 16, KW), I16),
            pltpu.VMEM((8, 16, QW), I16), pltpu.VMEM((8, 16, QW), I16),
            pltpu.VMEM((8, 16, KW), F32), pltpu.VMEM((8, 16, 1536), F32),
            pltpu.VMEM((8, 16, KW), I16), pltpu.VMEM((8, 16, QW), I16),
            pltpu.VMEM((7, 16, KW), I16), pltpu.VMEM((7, 16, QW), I16),
            pltpu.VMEM((8, 2, 16, 1536), BF16), pltpu.VMEM((2, 3, 4, 4, 16, KW), BF16),
            pltpu.VMEM((2, 4, 4, 5, 16, KW), BF16),
            pltpu.VMEM((7, 640, 512), BF16), pltpu.VMEM((7, 512, 640), BF16),
            pltpu.VMEM((4, 256, 256), BF16), pltpu.VMEM((2, 4, 640, 256), F32),
            pltpu.VMEM((4, 128, 256), F32), pltpu.VMEM((4, 1, 256), F32), pltpu.VMEM((4, 1, 256), F32),
            pltpu.SemaphoreType.DMA((copies,)), pltpu.SemaphoreType.DMA((copies,)), pltpu.SemaphoreType.DMA((10,)),
        ],
        compiler_params=pltpu.CompilerParams(
            collective_id=0, has_side_effects=True, vmem_limit_bytes=60 * 2**20
        ),
    )(
        positions, jnp.asarray(inv_row), jnp.asarray(inv_col), q_norm_gain, kv_norm_gain,
        hidden_in.T, w_qa, w_kva, w_qb, w_uk, value_up_weight,
    ).reshape(256, 512)


def solution(mesh):
    return jax.shard_map(
        body,
        mesh=mesh,
        in_specs=(
            P("seq", "head"), P("head", None), P("head", None), P(), P(), P(None, "head"),
            P("head", None, None), P("head", None, None), P("seq"),
        ),
        out_specs=P("seq", "head"),
        check_vma=False,
    )
```

```python
import functools
import math

import jax
import jax.numpy as jnp
import numpy as np
from jax import lax
from jax.experimental import pallas as pl
from jax.experimental.pallas import tpu as pltpu
from jax.sharding import PartitionSpec as P

MESH = pl.DeviceIdType.MESH
F32 = jnp.float32
BF16 = jnp.bfloat16
I16 = jnp.int16
BIG = 2.0**100
KW = 640
QW = 1536 + 128


def place():
    s = lax.axis_index("seq")
    h = lax.axis_index("head")
    return h % 2, ((h // 2) % 2) * 2 + s // 8, h // 4, s % 8


def device(core, x, y, z):
    return ((x % 2) * 8 + z, y * 4 + (x // 2) * 2 + core)


def dot(a, b, over_a=1, over_b=0):
    return lax.dot_general(a, b, (((over_a,), (over_b,)), ((), ())), preferred_element_type=F32)


def encode(values, width):
    rows = values.shape[0]
    top = jnp.maximum(jnp.max(jnp.abs(values), -1, keepdims=True), 2.0**-60)
    level = jnp.ceil(jnp.log2(top) * 512.0)
    digits = jnp.round(values * (jnp.exp2(level * (-1.0 / 512.0)) * 32700.0))
    return digits.astype(jnp.int32).astype(I16), jnp.broadcast_to(level, (rows, width)).astype(jnp.int32).astype(I16)


def decode(digits, level):
    unit = jnp.exp2(level.astype(jnp.int32).astype(F32) * (1.0 / 512.0)) * (1.0 / 32700.0)
    return digits.astype(jnp.int32).astype(F32) * unit


def kernel(
    pos_ref, row_hbm, col_hbm, qg_hbm, kg_hbm, hid_hbm, wqa_hbm, wkv_hbm, wqb_hbm, uk_hbm, up_hbm,
    out_ref,
    inv_row_ref, inv_col_ref, qg_ref, kg_ref, hid_t, wqa_ref, wkv_ref, wqb_ref, uk_ref, up_ref, hid, uk_t, up_t,
    sx_kv, rx_kv, sx_q, rx_q, own_kv, own_q, st_kv, st_q, rs_kv, rs_q,
    cq_ref, near_ref, far_ref, ke, vt, qt, s_ref, acc, m, l,
    send, recv, load,
):
    core, x, y, z = place()
    xh, xl = x // 2, x % 2
    j = y * 2 + xh
    p = x * (1 - core) + y * core
    q = y * (1 - core) + x * core
    used = [0]

    loads = []

    def fetch(*pairs):
        for src, dst in pairs:
            loads.append(pltpu.make_async_copy(src, dst, load.at[len(loads)]))
            loads[-1].start()

    fetch((hid_hbm, hid_t), (wkv_hbm, wkv_ref))

    def copy(src, dst, target):
        at = used[0]
        used[0] += 1
        done = pltpu.make_async_remote_copy(
            src_ref=src, dst_ref=dst, send_sem=send.at[at], recv_sem=recv.at[at],
            device_id=target, device_id_type=MESH,
        )
        done.start()
        return done

    sibling = device(1 - core, x, y, z)
    peers = []
    for dy, dx in ((0, 1), (1, 0), (1, 1), (2, 0), (2, 1), (3, 0), (3, 1)):
        py, px = (y + dy) % 4, (xh + dx) % 2
        peers.append((py * 2 + px, device(core, px * 2 + xl, py, z)))
    zs = [device(core, x, y, (z + d) % 8) for d in range(8)]
    order = range(1, 16)
    plane = [device(core, (x + d % 4) % 4, (y + d // 4) % 4, z) for d in order]
    barrier = pltpu.get_barrier_semaphore()
    greet = [sibling] + zs[1:] + plane
    for who in greet:
        pl.semaphore_signal(barrier, inc=1, device_id=who, device_id_type=MESH)

    loads[0].wait()
    rows = hid_t[...].T
    for h in range(16):
        hid[h % 2, 16 * (h // 2) : 16 * (h // 2) + 16] = rows[16 * h : 16 * h + 16]
    other = hid[1 - core]
    mine = hid[core]
    loads[1].wait()
    fetch((wqa_hbm, wqa_ref))
    digits, level = encode(dot(other, wkv_ref[...]), 64)
    sx_kv[:, :, :576] = digits.reshape(8, 16, 576)
    sx_kv[:, :, 576:] = level.reshape(8, 16, 64)
    pl.semaphore_wait(barrier, len(greet))
    c_kv = copy(sx_kv, rx_kv, sibling)
    loads[2].wait()
    digits, level = encode(dot(other, wqa_ref[...]), 128)
    sx_q[:, :, :1536] = digits.reshape(8, 16, 1536)
    sx_q[:, :, 1536:] = level.reshape(8, 16, 128)
    c_q = copy(sx_q, rx_q, sibling)
    fetch((uk_hbm, uk_ref), (up_hbm, up_ref), (qg_hbm, qg_ref), (kg_hbm, kg_ref), (row_hbm, inv_row_ref), (col_hbm, inv_col_ref))
    low = dot(mine, wkv_ref[...]).reshape(8, 16, 576)

    c_kv.wait()
    low = low + decode(rx_kv[:, :, :576], rx_kv[:, :, 576:577])
    own_kv[:, :, :576] = low
    own_kv[:, :, 576:] = jnp.zeros((8, 16, 64), F32)
    digits, level = encode(low.reshape(128, 576), 64)
    st_kv[:, :, :576] = digits.reshape(8, 16, 576)
    st_kv[:, :, 576:] = level.reshape(8, 16, 64)
    p_kv = [copy(st_kv.at[pj], rs_kv.at[i], who) for i, (pj, who) in enumerate(peers)]
    low = dot(mine, wqa_ref[...]).reshape(8, 16, 1536)
    c_q.wait()
    low = low + decode(rx_q[:, :, :1536], rx_q[:, :, 1536:1537])
    own_q[...] = low
    digits, level = encode(low.reshape(128, 1536), 128)
    st_q[:, :, :1536] = digits.reshape(8, 16, 1536)
    st_q[:, :, 1536:] = level.reshape(8, 16, 128)
    p_q = [copy(st_q.at[pj], rs_q.at[i], who) for i, (pj, who) in enumerate(peers)]

    fetch((wqb_hbm, wqb_ref))

    h = j * 2 + core
    base = pos_ref[128 * (h // 8)]
    run = base // 128
    tok = (base + (h % 8) * 16 + lax.broadcasted_iota(jnp.int32, (16, 128), 0)).astype(F32)
    lane = lax.broadcasted_iota(jnp.int32, (16, 128), 1)
    for i in range(3, 9):
        loads[i].wait()
    angle = tok * inv_row_ref[...]
    cosine, sine = jnp.cos(angle), jnp.sin(angle)
    tail = jnp.where(lane < 96, jnp.where(run > lane - 64, -BIG, 0.0), 0.0)
    for i in range(4):
        uk_t[:, 128 * i : 128 * i + 128] = uk_ref[i].T
        up_t[128 * i : 128 * i + 128, :] = up_ref[i].T
    for c in p_kv:
        c.wait()
    low = own_kv[j]
    parts = [decode(rs_kv[i, :, :576], rs_kv[i, :, 576:577]) for i in range(7)]
    latent = low[:, :512] + sum(part[:, :512] for part in parts)
    latent = latent * lax.rsqrt(jnp.mean(latent * latent, -1, keepdims=True) + 1e-06) * kg_ref[...].reshape(1, 512)
    near_ref[core, 0, p, q, :, :512] = latent.astype(BF16)
    rope = sum(part[:, 512:576] for part in parts)
    rope = low[:, 512:] + jnp.concatenate([rope, jnp.zeros((16, 64), F32)], 1)
    swapped = jnp.where(lane < 32, -pltpu.roll(rope, 96, 1), pltpu.roll(rope, 32, 1))
    rope = jnp.where(lane < 64, rope * cosine + swapped * sine, tail)
    near_ref[core, 0, p, q, :, 512:] = rope.astype(BF16)
    block = near_ref.at[core, 0, p, q]
    p_z = [copy(block, far_ref.at[core, p, q, d - 2], zs[d]) for d in (2, 6, 3, 5, 4)]
    p_p = [copy(block, block, who) for who in plane]

    for c in p_q:
        c.wait()
    low = own_q[j]
    for i in range(7):
        low = low + decode(rs_q[i, :, :1536], rs_q[i, :, 1536:1537])
    low = low * lax.rsqrt(jnp.mean(low * low, -1, keepdims=True) + 1e-06) * qg_ref[...].reshape(1, 1536)
    cq_ref[j, core] = low.astype(BF16)
    block = cq_ref.at[j, core]
    p_c = [copy(block, block, who) for _, who in peers]

    def share(part):
        return copy(part, part, sibling)

    for c in p_z:
        c.wait()

    def spread(a, steps):
        part = far_ref.at[core, (p + a) % 4, q]
        return [
            copy(part, part, device(
                core, (x + da * (1 - core) + db * core) % 4, (y + da * core + db * (1 - core)) % 4, z,
            ))
            for da, db in steps
        ]

    across = ((0, 1), (0, 3), (0, 2))
    first = spread(0, ((1, 0), (3, 0), (2, 0)))
    lines = {0: spread(0, across)}
    s_lines = {}

    for c in p_p:
        c.wait()
    mine = near_ref.at[core, 0]
    beside = [copy(mine, near_ref.at[core, 1], zs[1]), copy(mine, near_ref.at[core, 2], zs[7])]
    s_near = [share(mine)]

    def finish(a):
        for c in lines[a]:
            c.wait()
        s_lines[a] = share(far_ref.at[core, (p + a) % 4])

    sp = y * (1 - core) + x * core
    scale = math.log2(math.e) / math.sqrt(192)

    def near_keys(r, cols):
        return near_ref[:, r, :, :, :, cols].reshape(512, -1)

    def far_keys(a, cols):
        return jnp.concatenate([
            far_ref[core, (p + a) % 4, :, :, :, cols].reshape(320, -1),
            far_ref[1 - core, (sp + a) % 4, :, :, :, cols].reshape(320, -1),
        ], 0)

    def expand(n, keys, which):
        keys = keys(which, slice(0, 512))
        count = keys.shape[0]
        ke[n, :count] = (dot(keys, uk_t[...]) * scale).astype(BF16)
        vt[n, :, :count] = dot(up_t[...], keys, 1, 1).astype(BF16)

    def score(n, keys, which, i, diagonal=False):
        tails = keys(which, slice(512, KW))
        count = tails.shape[0]
        s_ref[n % 2, i, :count] = dot(jnp.concatenate([ke[n, :count, 128 * i : 128 * i + 128], tails], 1), qt[i])
        if diagonal:
            at = lax.broadcasted_iota(jnp.int32, (16, 256), 1)
            token = at % 128 // 16 * 32 + at // 128 * 16 + at % 16
            row = lax.broadcasted_iota(jnp.int32, (16, 256), 0)
            for k in range(2):
                for ky in range(4):
                    for half in range(2):
                        at = (ky * 4 + xl + 2 * half) if k else ((xl + 2 * half) * 4 + ky)
                        strip = pl.ds(pl.multiple_of(k * 256 + at * 16, 16), 16)
                        key_token = (ky * 4 + half * 2 + k) * 16 + row
                        hidden = (key_token > token) & (key_token // 128 == token // 128)
                        s_ref[n % 2, i, strip] = jnp.where(hidden, -BIG, s_ref[n % 2, i, strip])

    def weigh(n, count, i):
        s = s_ref[n % 2, i, :count]
        before = m[i]
        now = jnp.maximum(before, jnp.max(s, 0, keepdims=True))
        w = jnp.exp2(s - now)
        fade = jnp.exp2(before - now)
        l[i] = l[i] * fade + jnp.sum(w, 0, keepdims=True)
        m[i] = now
        acc[i] = acc[i] * fade + dot(vt[n, 128 * i : 128 * i + 128, :count], w.astype(BF16))

    def step(n, count, keys, which):
        for i in range(4):
            score(n, keys, which, i)
            weigh(n - 1, count, i)

    m[...] = jnp.full(m.shape, -4 * BIG, F32)
    l[...] = jnp.zeros(l.shape, F32)
    acc[...] = jnp.zeros(acc.shape, F32)

    def queries(k):
        wide = lax.broadcasted_iota(jnp.int32, (32, 128), 1)
        base = jnp.where(wide < 64, pos_ref[0], pos_ref[128])
        angle = (base + wide % 64 // 16 * 32 + k * 16 + wide % 16).astype(F32) * inv_col_ref[...]
        cosine, sine = jnp.cos(angle), jnp.sin(angle)
        runs = jnp.where(base // 128 == lax.broadcasted_iota(jnp.int32, (32, 128), 0), 1.0, 0.0).astype(BF16)
        at = pl.ds(pl.multiple_of(k * 128, 128), 128)
        q_t = dot(cq_ref[:, pl.ds(k, 1)].reshape(128, 1536), wqb_ref[...]).astype(BF16).T
        for i in range(4):
            qt[i, :128, at] = q_t[192 * i : 192 * i + 128]
            a = q_t[192 * i + 128 : 192 * i + 160].astype(F32)
            b = q_t[192 * i + 160 : 192 * i + 192].astype(F32)
            qt[i, 128:160, at] = ((a * cosine - b * sine) * scale).astype(BF16)
            qt[i, 160:192, at] = ((b * cosine + a * sine) * scale).astype(BF16)
            qt[i, 192:224, at] = runs
            qt[i, 224:, at] = jnp.zeros((32, 128), BF16)

    s_near[0].wait()
    expand(0, near_keys, 0)
    for c in p_c:
        c.wait()
    mate = cq_ref.at[:, pl.ds(core, 1)]
    c_c = share(mate)
    for n, a in ((0, 3), (1, 1), (2, 2)):
        first[n].wait()
        lines[a] = spread(a, across)
    loads[9].wait()
    queries(core)
    finish(0)
    c_c.wait()
    queries(1 - core)
    for r in (1, 2):
        beside[r - 1].wait()
        s_near.append(share(near_ref.at[core, r]))
    for i in range(4):
        score(0, near_keys, 0, i, True)
    s_lines[0].wait()
    expand(1, far_keys, 0)
    step(1, 512, far_keys, 0)
    finish(3)
    s_near[1].wait()
    expand(2, near_keys, 1)
    step(2, 640, near_keys, 1)
    s_near[2].wait()
    expand(3, near_keys, 2)
    step(3, 512, near_keys, 2)
    finish(1)
    s_lines[3].wait()
    expand(4, far_keys, 3)
    step(4, 512, far_keys, 3)
    s_lines[1].wait()
    expand(5, far_keys, 1)
    finish(2)
    step(5, 640, far_keys, 1)
    s_lines[2].wait()
    expand(6, far_keys, 2)
    step(6, 640, far_keys, 2)
    for i in range(4):
        weigh(6, 640, i)
    for i in range(4):
        values = (acc[i] / l[i]).T.astype(BF16)
        for k in range(2):
            out_ref[:, k, :, 128 * i : 128 * i + 128] = values[128 * k : 128 * k + 128].reshape(8, 16, 128)


def body(hidden_in, w_qa, w_kva, q_norm_gain, kv_norm_gain, w_qb, w_uk, value_up_weight, positions):
    inverse = 50000.0 ** (-np.arange(0, 64, 2) / 64)
    inv_row = np.zeros((1, 128), np.float32)
    inv_row[0, :32] = inverse
    inv_row[0, 32:64] = inverse
    inv_col = np.repeat(inverse.astype(np.float32)[:, None], 128, 1)
    vmem = pl.BlockSpec(memory_space=pltpu.VMEM)
    smem = pl.BlockSpec(memory_space=pltpu.SMEM)
    any_space = pl.BlockSpec(memory_space=pl.ANY)
    copies = 80
    return pl.pallas_call(
        kernel,
        name="attention",
        out_shape=pltpu.VMEM((8, 2, 16, 512), BF16),
        in_specs=[smem] + [any_space] * 10,
        out_specs=vmem,
        scratch_shapes=[
            pltpu.VMEM((1, 128), F32), pltpu.VMEM((32, 128), F32), pltpu.VMEM((1536,), F32), pltpu.VMEM((512,), F32),
            pltpu.VMEM((448, 256), BF16), pltpu.VMEM((448, 1536), BF16), pltpu.VMEM((448, 576), BF16),
            pltpu.VMEM((1536, 768), BF16), pltpu.VMEM((4, 128, 512), BF16), pltpu.VMEM((4, 512, 128), BF16),
            pltpu.VMEM((2, 128, 448), BF16), pltpu.VMEM((512, 512), BF16), pltpu.VMEM((512, 512), BF16),
            pltpu.VMEM((8, 16, KW), I16), pltpu.VMEM((8, 16, KW), I16),
            pltpu.VMEM((8, 16, QW), I16), pltpu.VMEM((8, 16, QW), I16),
            pltpu.VMEM((8, 16, KW), F32), pltpu.VMEM((8, 16, 1536), F32),
            pltpu.VMEM((8, 16, KW), I16), pltpu.VMEM((8, 16, QW), I16),
            pltpu.VMEM((7, 16, KW), I16), pltpu.VMEM((7, 16, QW), I16),
            pltpu.VMEM((8, 2, 16, 1536), BF16), pltpu.VMEM((2, 3, 4, 4, 16, KW), BF16),
            pltpu.VMEM((2, 4, 4, 5, 16, KW), BF16),
            pltpu.VMEM((7, 640, 512), BF16), pltpu.VMEM((7, 512, 640), BF16),
            pltpu.VMEM((4, 256, 256), BF16), pltpu.VMEM((2, 4, 640, 256), F32),
            pltpu.VMEM((4, 128, 256), F32), pltpu.VMEM((4, 1, 256), F32), pltpu.VMEM((4, 1, 256), F32),
            pltpu.SemaphoreType.DMA((copies,)), pltpu.SemaphoreType.DMA((copies,)), pltpu.SemaphoreType.DMA((10,)),
        ],
        compiler_params=pltpu.CompilerParams(
            collective_id=0, has_side_effects=True, vmem_limit_bytes=60 * 2**20
        ),
    )(
        positions, jnp.asarray(inv_row), jnp.asarray(inv_col), q_norm_gain, kv_norm_gain,
        hidden_in.T, w_qa, w_kva, w_qb, w_uk, value_up_weight,
    ).reshape(256, 512)


def solution(mesh):
    return jax.shard_map(
        body,
        mesh=mesh,
        in_specs=(
            P("seq", "head"), P("head", None), P("head", None), P(), P(), P(None, "head"),
            P("head", None, None), P("head", None, None), P("seq"),
        ),
        out_specs=P("seq", "head"),
        check_vma=False,
    )
```

```python
import functools
import math

import jax
import jax.numpy as jnp
import numpy as np
from jax import lax
from jax.experimental import pallas as pl
from jax.experimental.pallas import tpu as pltpu
from jax.sharding import PartitionSpec as P

MESH = pl.DeviceIdType.MESH
F32 = jnp.float32
BF16 = jnp.bfloat16
I16 = jnp.int16
BIG = 2.0**100
KW = 640
QW = 1536 + 128


def place():
    s = lax.axis_index("seq")
    h = lax.axis_index("head")
    return h % 2, ((h // 2) % 2) * 2 + s // 8, h // 4, s % 8


def device(core, x, y, z):
    return ((x % 2) * 8 + z, y * 4 + (x // 2) * 2 + core)


def dot(a, b, over_a=1, over_b=0):
    return lax.dot_general(a, b, (((over_a,), (over_b,)), ((), ())), preferred_element_type=F32)


def encode(values, width):
    rows = values.shape[0]
    top = jnp.maximum(jnp.max(jnp.abs(values), -1, keepdims=True), 2.0**-60)
    level = jnp.ceil(jnp.log2(top) * 512.0)
    digits = jnp.round(values * (jnp.exp2(level * (-1.0 / 512.0)) * 32700.0))
    return digits.astype(jnp.int32).astype(I16), jnp.broadcast_to(level, (rows, width)).astype(jnp.int32).astype(I16)


def decode(digits, level):
    unit = jnp.exp2(level.astype(jnp.int32).astype(F32) * (1.0 / 512.0)) * (1.0 / 32700.0)
    return digits.astype(jnp.int32).astype(F32) * unit


def kernel(
    pos_ref, row_hbm, col_hbm, qg_hbm, kg_hbm, hid_hbm, wqa_hbm, wkv_hbm, wqb_hbm, uk_hbm, up_hbm,
    out_ref,
    inv_row_ref, inv_col_ref, qg_ref, kg_ref, hid_t, wqa_ref, wkv_ref, wqb_ref, uk_ref, up_ref, hid, uk_t, up_t,
    sx_kv, rx_kv, sx_q, rx_q, own_kv, own_q, st_kv, st_q, rs_kv, rs_q,
    cq_ref, near_ref, far_ref, ke, vt, qt, s_ref, acc, m, l,
    send, recv, load,
):
    core, x, y, z = place()
    xh, xl = x // 2, x % 2
    j = y * 2 + xh
    p = x * (1 - core) + y * core
    q = y * (1 - core) + x * core
    used = [0]

    loads = []

    def fetch(*pairs):
        for src, dst in pairs:
            loads.append(pltpu.make_async_copy(src, dst, load.at[len(loads)]))
            loads[-1].start()

    fetch((hid_hbm, hid_t), (wkv_hbm, wkv_ref))

    def copy(src, dst, target):
        at = used[0]
        used[0] += 1
        done = pltpu.make_async_remote_copy(
            src_ref=src, dst_ref=dst, send_sem=send.at[at], recv_sem=recv.at[at],
            device_id=target, device_id_type=MESH,
        )
        done.start()
        return done

    sibling = device(1 - core, x, y, z)
    peers = []
    for dy, dx in ((0, 1), (1, 0), (1, 1), (2, 0), (2, 1), (3, 0), (3, 1)):
        py, px = (y + dy) % 4, (xh + dx) % 2
        peers.append((py * 2 + px, device(core, px * 2 + xl, py, z)))
    zs = [device(core, x, y, (z + d) % 8) for d in range(8)]
    order = range(1, 16)
    plane = [device(core, (x + d % 4) % 4, (y + d // 4) % 4, z) for d in order]
    barrier = pltpu.get_barrier_semaphore()
    greet = [sibling] + zs[1:] + plane
    for who in greet:
        pl.semaphore_signal(barrier, inc=1, device_id=who, device_id_type=MESH)

    loads[0].wait()
    rows = hid_t[...].T
    for h in range(16):
        hid[h % 2, 16 * (h // 2) : 16 * (h // 2) + 16] = rows[16 * h : 16 * h + 16]
    other = hid[1 - core]
    mine = hid[core]
    loads[1].wait()
    fetch((wqa_hbm, wqa_ref))
    digits, level = encode(dot(other, wkv_ref[...]), 64)
    sx_kv[:, :, :576] = digits.reshape(8, 16, 576)
    sx_kv[:, :, 576:] = level.reshape(8, 16, 64)
    pl.semaphore_wait(barrier, len(greet))
    c_kv = copy(sx_kv, rx_kv, sibling)
    loads[2].wait()
    digits, level = encode(dot(other, wqa_ref[...]), 128)
    sx_q[:, :, :1536] = digits.reshape(8, 16, 1536)
    sx_q[:, :, 1536:] = level.reshape(8, 16, 128)
    c_q = copy(sx_q, rx_q, sibling)
    fetch((uk_hbm, uk_ref), (up_hbm, up_ref), (qg_hbm, qg_ref), (kg_hbm, kg_ref), (row_hbm, inv_row_ref), (col_hbm, inv_col_ref))
    low = dot(mine, wkv_ref[...]).reshape(8, 16, 576)

    c_kv.wait()
    low = low + decode(rx_kv[:, :, :576], rx_kv[:, :, 576:577])
    own_kv[:, :, :576] = low
    own_kv[:, :, 576:] = jnp.zeros((8, 16, 64), F32)
    digits, level = encode(low.reshape(128, 576), 64)
    st_kv[:, :, :576] = digits.reshape(8, 16, 576)
    st_kv[:, :, 576:] = level.reshape(8, 16, 64)
    p_kv = [copy(st_kv.at[pj], rs_kv.at[i], who) for i, (pj, who) in enumerate(peers)]
    low = dot(mine, wqa_ref[...]).reshape(8, 16, 1536)
    c_q.wait()
    low = low + decode(rx_q[:, :, :1536], rx_q[:, :, 1536:1537])
    own_q[...] = low
    digits, level = encode(low.reshape(128, 1536), 128)
    st_q[:, :, :1536] = digits.reshape(8, 16, 1536)
    st_q[:, :, 1536:] = level.reshape(8, 16, 128)
    p_q = [copy(st_q.at[pj], rs_q.at[i], who) for i, (pj, who) in enumerate(peers)]

    fetch((wqb_hbm, wqb_ref))

    h = j * 2 + core
    base = pos_ref[128 * (h // 8)]
    run = base // 128
    tok = (base + (h % 8) * 16 + lax.broadcasted_iota(jnp.int32, (16, 128), 0)).astype(F32)
    lane = lax.broadcasted_iota(jnp.int32, (16, 128), 1)
    for i in range(3, 9):
        loads[i].wait()
    angle = tok * inv_row_ref[...]
    cosine, sine = jnp.cos(angle), jnp.sin(angle)
    tail = jnp.where(lane < 96, jnp.where(run > lane - 64, -BIG, 0.0), 0.0)
    for i in range(4):
        uk_t[:, 128 * i : 128 * i + 128] = uk_ref[i].T
        up_t[128 * i : 128 * i + 128, :] = up_ref[i].T
    for c in p_kv:
        c.wait()
    low = own_kv[j]
    parts = [decode(rs_kv[i, :, :576], rs_kv[i, :, 576:577]) for i in range(7)]
    latent = low[:, :512] + sum(part[:, :512] for part in parts)
    latent = latent * lax.rsqrt(jnp.mean(latent * latent, -1, keepdims=True) + 1e-06) * kg_ref[...].reshape(1, 512)
    near_ref[core, 0, p, q, :, :512] = latent.astype(BF16)
    rope = sum(part[:, 512:576] for part in parts)
    rope = low[:, 512:] + jnp.concatenate([rope, jnp.zeros((16, 64), F32)], 1)
    swapped = jnp.where(lane < 32, -pltpu.roll(rope, 96, 1), pltpu.roll(rope, 32, 1))
    rope = jnp.where(lane < 64, rope * cosine + swapped * sine, tail)
    near_ref[core, 0, p, q, :, 512:] = rope.astype(BF16)
    block = near_ref.at[core, 0, p, q]
    p_z = [copy(block, far_ref.at[core, p, q, d - 2], zs[d]) for d in (2, 6, 3, 5, 4)]
    p_p = [copy(block, block, who) for who in plane]

    for c in p_q:
        c.wait()
    low = own_q[j]
    for i in range(7):
        low = low + decode(rs_q[i, :, :1536], rs_q[i, :, 1536:1537])
    low = low * lax.rsqrt(jnp.mean(low * low, -1, keepdims=True) + 1e-06) * qg_ref[...].reshape(1, 1536)
    cq_ref[j, core] = low.astype(BF16)
    block = cq_ref.at[j, core]
    p_c = [copy(block, block, who) for _, who in peers]

    def share(part):
        return copy(part, part, sibling)

    for c in p_z:
        c.wait()

    def spread(a, steps):
        part = far_ref.at[core, (p + a) % 4, q]
        return [
            copy(part, part, device(
                core, (x + da * (1 - core) + db * core) % 4, (y + da * core + db * (1 - core)) % 4, z,
            ))
            for da, db in steps
        ]

    across = ((0, 1), (0, 3), (0, 2))
    first = spread(0, ((1, 0), (3, 0), (2, 0)))
    lines = {0: spread(0, across)}
    s_lines = {}

    for c in p_p:
        c.wait()
    mine = near_ref.at[core, 0]
    beside = [copy(mine, near_ref.at[core, 1], zs[1]), copy(mine, near_ref.at[core, 2], zs[7])]
    s_near = [share(mine)]

    def finish(a):
        for c in lines[a]:
            c.wait()
        s_lines[a] = share(far_ref.at[core, (p + a) % 4])

    def finish_last(a):
        s_lines[a] = [share(far_ref.at[core, (p + a) % 4, q])]
        for c, b in zip(lines[a], (3, 1, 2)):
            c.wait()
            s_lines[a].append(share(far_ref.at[core, (p + a) % 4, (q + b) % 4]))

    sp = y * (1 - core) + x * core
    scale = math.log2(math.e) / math.sqrt(192)

    def near_keys(r, cols):
        return near_ref[:, r, :, :, :, cols].reshape(512, -1)

    def far_keys(a, cols):
        return jnp.concatenate([
            far_ref[core, (p + a) % 4, :, :, :, cols].reshape(320, -1),
            far_ref[1 - core, (sp + a) % 4, :, :, :, cols].reshape(320, -1),
        ], 0)

    def expand(n, keys, which):
        keys = keys(which, slice(0, 512))
        count = keys.shape[0]
        ke[n, :count] = (dot(keys, uk_t[...]) * scale).astype(BF16)
        vt[n, :, :count] = dot(up_t[...], keys, 1, 1).astype(BF16)

    def score(n, keys, which, i, diagonal=False):
        tails = keys(which, slice(512, KW))
        count = tails.shape[0]
        s_ref[n % 2, i, :count] = dot(jnp.concatenate([ke[n, :count, 128 * i : 128 * i + 128], tails], 1), qt[i])
        if diagonal:
            at = lax.broadcasted_iota(jnp.int32, (16, 256), 1)
            token = at % 128 // 16 * 32 + at // 128 * 16 + at % 16
            row = lax.broadcasted_iota(jnp.int32, (16, 256), 0)
            for k in range(2):
                for ky in range(4):
                    for half in range(2):
                        at = (ky * 4 + xl + 2 * half) if k else ((xl + 2 * half) * 4 + ky)
                        strip = pl.ds(pl.multiple_of(k * 256 + at * 16, 16), 16)
                        key_token = (ky * 4 + half * 2 + k) * 16 + row
                        hidden = (key_token > token) & (key_token // 128 == token // 128)
                        s_ref[n % 2, i, strip] = jnp.where(hidden, -BIG, s_ref[n % 2, i, strip])

    def weigh(n, count, i):
        s = s_ref[n % 2, i, :count]
        before = m[i]
        now = jnp.maximum(before, jnp.max(s, 0, keepdims=True))
        w = jnp.exp2(s - now)
        fade = jnp.exp2(before - now)
        l[i] = l[i] * fade + jnp.sum(w, 0, keepdims=True)
        m[i] = now
        acc[i] = acc[i] * fade + dot(vt[n, 128 * i : 128 * i + 128, :count], w.astype(BF16))

    def step(n, count, keys, which):
        for i in range(4):
            score(n, keys, which, i)
            weigh(n - 1, count, i)

    m[...] = jnp.full(m.shape, -4 * BIG, F32)
    l[...] = jnp.zeros(l.shape, F32)
    acc[...] = jnp.zeros(acc.shape, F32)

    def queries(k):
        wide = lax.broadcasted_iota(jnp.int32, (32, 128), 1)
        base = jnp.where(wide < 64, pos_ref[0], pos_ref[128])
        angle = (base + wide % 64 // 16 * 32 + k * 16 + wide % 16).astype(F32) * inv_col_ref[...]
        cosine, sine = jnp.cos(angle), jnp.sin(angle)
        runs = jnp.where(base // 128 == lax.broadcasted_iota(jnp.int32, (32, 128), 0), 1.0, 0.0).astype(BF16)
        at = pl.ds(pl.multiple_of(k * 128, 128), 128)
        q_t = dot(cq_ref[:, pl.ds(k, 1)].reshape(128, 1536), wqb_ref[...]).astype(BF16).T
        for i in range(4):
            qt[i, :128, at] = q_t[192 * i : 192 * i + 128]
            a = q_t[192 * i + 128 : 192 * i + 160].astype(F32)
            b = q_t[192 * i + 160 : 192 * i + 192].astype(F32)
            qt[i, 128:160, at] = ((a * cosine - b * sine) * scale).astype(BF16)
            qt[i, 160:192, at] = ((b * cosine + a * sine) * scale).astype(BF16)
            qt[i, 192:224, at] = runs
            qt[i, 224:, at] = jnp.zeros((32, 128), BF16)

    s_near[0].wait()
    expand(0, near_keys, 0)
    for c in p_c:
        c.wait()
    mate = cq_ref.at[:, pl.ds(core, 1)]
    c_c = share(mate)
    for n, a in ((0, 3), (1, 1), (2, 2)):
        first[n].wait()
        lines[a] = spread(a, across)
    loads[9].wait()
    queries(core)
    finish(0)
    c_c.wait()
    queries(1 - core)
    for r in (1, 2):
        beside[r - 1].wait()
        s_near.append(share(near_ref.at[core, r]))
    for i in range(4):
        score(0, near_keys, 0, i, True)
    s_lines[0].wait()
    expand(1, far_keys, 0)
    step(1, 512, far_keys, 0)
    finish(3)
    s_near[1].wait()
    expand(2, near_keys, 1)
    step(2, 640, near_keys, 1)
    s_near[2].wait()
    expand(3, near_keys, 2)
    step(3, 512, near_keys, 2)
    finish(1)
    s_lines[3].wait()
    expand(4, far_keys, 3)
    step(4, 512, far_keys, 3)
    s_lines[1].wait()
    expand(5, far_keys, 1)
    finish_last(2)
    step(5, 640, far_keys, 1)
    for i in range(4):
        weigh(5, 640, i)
    for c in s_lines[2]:
        c.wait()
    expand(6, far_keys, 2)
    for i in range(4):
        score(6, far_keys, 2, i)
    for i in range(4):
        weigh(6, 640, i)
    for i in range(4):
        values = (acc[i] / l[i]).T.astype(BF16)
        for k in range(2):
            out_ref[:, k, :, 128 * i : 128 * i + 128] = values[128 * k : 128 * k + 128].reshape(8, 16, 128)


def body(hidden_in, w_qa, w_kva, q_norm_gain, kv_norm_gain, w_qb, w_uk, value_up_weight, positions):
    inverse = 50000.0 ** (-np.arange(0, 64, 2) / 64)
    inv_row = np.zeros((1, 128), np.float32)
    inv_row[0, :32] = inverse
    inv_row[0, 32:64] = inverse
    inv_col = np.repeat(inverse.astype(np.float32)[:, None], 128, 1)
    vmem = pl.BlockSpec(memory_space=pltpu.VMEM)
    smem = pl.BlockSpec(memory_space=pltpu.SMEM)
    any_space = pl.BlockSpec(memory_space=pl.ANY)
    copies = 80
    return pl.pallas_call(
        kernel,
        name="attention",
        out_shape=pltpu.VMEM((8, 2, 16, 512), BF16),
        in_specs=[smem] + [any_space] * 10,
        out_specs=vmem,
        scratch_shapes=[
            pltpu.VMEM((1, 128), F32), pltpu.VMEM((32, 128), F32), pltpu.VMEM((1536,), F32), pltpu.VMEM((512,), F32),
            pltpu.VMEM((448, 256), BF16), pltpu.VMEM((448, 1536), BF16), pltpu.VMEM((448, 576), BF16),
            pltpu.VMEM((1536, 768), BF16), pltpu.VMEM((4, 128, 512), BF16), pltpu.VMEM((4, 512, 128), BF16),
            pltpu.VMEM((2, 128, 448), BF16), pltpu.VMEM((512, 512), BF16), pltpu.VMEM((512, 512), BF16),
            pltpu.VMEM((8, 16, KW), I16), pltpu.VMEM((8, 16, KW), I16),
            pltpu.VMEM((8, 16, QW), I16), pltpu.VMEM((8, 16, QW), I16),
            pltpu.VMEM((8, 16, KW), F32), pltpu.VMEM((8, 16, 1536), F32),
            pltpu.VMEM((8, 16, KW), I16), pltpu.VMEM((8, 16, QW), I16),
            pltpu.VMEM((7, 16, KW), I16), pltpu.VMEM((7, 16, QW), I16),
            pltpu.VMEM((8, 2, 16, 1536), BF16), pltpu.VMEM((2, 3, 4, 4, 16, KW), BF16),
            pltpu.VMEM((2, 4, 4, 5, 16, KW), BF16),
            pltpu.VMEM((7, 640, 512), BF16), pltpu.VMEM((7, 512, 640), BF16),
            pltpu.VMEM((4, 256, 256), BF16), pltpu.VMEM((2, 4, 640, 256), F32),
            pltpu.VMEM((4, 128, 256), F32), pltpu.VMEM((4, 1, 256), F32), pltpu.VMEM((4, 1, 256), F32),
            pltpu.SemaphoreType.DMA((copies,)), pltpu.SemaphoreType.DMA((copies,)), pltpu.SemaphoreType.DMA((10,)),
        ],
        compiler_params=pltpu.CompilerParams(
            collective_id=0, has_side_effects=True, vmem_limit_bytes=60 * 2**20
        ),
    )(
        positions, jnp.asarray(inv_row), jnp.asarray(inv_col), q_norm_gain, kv_norm_gain,
        hidden_in.T, w_qa, w_kva, w_qb, w_uk, value_up_weight,
    ).reshape(256, 512)


def solution(mesh):
    return jax.shard_map(
        body,
        mesh=mesh,
        in_specs=(
            P("seq", "head"), P("head", None), P("head", None), P(), P(), P(None, "head"),
            P("head", None, None), P("head", None, None), P("seq"),
        ),
        out_specs=P("seq", "head"),
        check_vma=False,
    )
```
